256 devices in a mesh: inst: 64 (over y, z, core), head: 4 (over x).
Axes of the slice: x: 4, y: 4, z: 8, core: 2. Of those that a mesh axis runs over, the one named last changes fastest.
Arguments:
- queries: bfloat16 [64, 128, 3072], P('inst', None, 'head'), may hold values from -240 to 240
- new_keys: bfloat16 [64, 128, 3072], P('inst', None, 'head'), may hold values from -6 to 6
- new_values: bfloat16 [64, 128, 3072], P('inst', None, 'head'), may hold values from -6 to 6
- pool: bfloat16 [384, 128, 6144], P(None, 'inst', 'head'), may hold values from -6 to 6
- block_table: int32 [384], replicated, may hold values from 0 to 383, each once
- block_counts: int32 [64], replicated, may hold values from 1 to 6, 224 in all
- key_weight: bfloat16 [6144, 3072], P('inst', 'head'), may hold values from -0.078125 to 0.078125
- value_weight: bfloat16 [6144, 3072], P('inst', 'head'), may hold values from -0.078125 to 0.078125
Outputs:
- attention: bfloat16 [64, 128, 3072], P('inst', None, 'head')
The draws below stay inside these ranges and needn't reach their ends.
Inputs may be any that keep to these rules, and one draw needn't show every extreme that they name: Every entry of block_table names a distinct pool block; conversation c uses the first block_counts[c] of its 6 entries. `block_counts`: the counts of all conversations sum to exactly 224, and some conversation has exactly 6 blocks.
All inputs are finite; a program needn't handle non-finite values.
Results may differ from the reference program's by a relative error of at most 0.0064.
Values may be sent and summed in bfloat16 or wider, within the bound.
No kernel may reach another device: no remote copies, remote signals or barrier semaphores. Data moves between devices by JAX's collectives and lax.ppermute only.
A program may use at most 128 MiB of HBM per device.

```python
import math
import jax
import jax.numpy as jnp
import numpy as np
from jax import lax

D = 6144
HEADS = 48
HD = 64
BLOCK = 128
MAXB = 6
NEW = 128
CONV = 64
POOL_BLK = 384
USED = 224


def shared_base(key):
    return jnp.clip(jax.random.normal(key, (CONV, NEW, HEADS * HD), jnp.float32), -6.0, 6.0)


def draw_queries(key, part):
    key = jax.random.fold_in(key, 11)
    fresh = jnp.clip(jax.random.normal(key, (CONV, NEW, HEADS * HD), jnp.float32), -6.0, 6.0)
    return fresh.astype(jnp.bfloat16)


def draw_new_keys(key, part):
    base = shared_base(key)
    return base.astype(jnp.bfloat16)


def level_of(own_key, dims, cuts, smallest, top_value):
    gain = 1.0
    for position, shards_of in cuts:
        steps = jax.random.uniform(jax.random.fold_in(jax.random.fold_in(own_key, 6), position), (shards_of,), jnp.float32, smallest / len(cuts), top_value / len(cuts))
        gain = gain * jnp.repeat(jnp.exp(steps), dims[position] // shards_of).reshape((-1,) + (1,) * (len(dims) - 1 - position))
    return gain


def profile(amount, total, most, lean):
    loads = [(1 << 20) // math.isqrt(rank ** lean) + 1 for rank in range(2, amount + 1)]
    rest, counts = total - most - (amount - 1), [1] * (amount - 1)
    while rest > 0:
        candidates = [i for i in range(amount - 1) if counts[i] < most]
        mass, left = sum([loads[i] for i in candidates]), rest
        for i in candidates:
            addition = min(most - counts[i], max(1, left * loads[i] // mass), rest)
            counts[i] = counts[i] + addition
            rest = rest - addition
    return np.array([most] + counts)


def uneven(rng, amount, total, limit, slope):
    if amount == 2:
        one = jax.random.randint(rng, (), max(1, total - limit), min(limit, total - 1) + 1)
        return jnp.stack([one, total - one])
    lengths = jnp.asarray(profile(amount, total, limit, slope), jnp.int32)
    pairs = (amount - 1) // 2
    source_of, receiver = lengths[1:1 + 2 * pairs:2], lengths[2:2 + 2 * pairs:2]
    room = jnp.minimum(source_of - 1, limit - receiver)
    passed = jax.random.randint(jax.random.fold_in(rng, 1), (pairs,), 0, 1 << 20) % (room + 1)
    lengths = lengths.at[1:1 + 2 * pairs:2].set(source_of - passed).at[2:2 + 2 * pairs:2].set(receiver + passed)
    return lengths[jax.random.permutation(jax.random.fold_in(rng, 2), amount)]


def bell_draw(own_key, dims, deviation, reach, pieces=(), held_as=jnp.bfloat16):
    values = deviation * jax.random.normal(own_key, dims, jnp.float32)
    if pieces:
        values = values * level_of(own_key, dims, pieces, -0.22, 0.18)
    return jnp.clip(values, -reach, reach).astype(held_as)


def setup_inputs(seed: int = 0) -> dict:
    splits = jax.random.split(jax.random.key(seed), 9)
    queries = draw_queries(jax.random.fold_in(splits[8], 71), 0)
    new_keys = draw_new_keys(jax.random.fold_in(splits[8], 71), 0)
    new_values = bell_draw(splits[2], (CONV, NEW, HEADS * HD), 1.0, 6.0, ((0, 64), (2, 4)))
    pool = bell_draw(splits[3], (POOL_BLK, BLOCK, D), 1.0, 6.0, ((1, 64), (2, 4)))
    block_table = jax.random.permutation(splits[4], POOL_BLK).astype(jnp.int32)
    block_counts = uneven(splits[5], CONV, USED, MAXB, 2).astype(jnp.int32)
    key_weight = bell_draw(splits[6], (D, HEADS * HD), D ** -0.5, 0.078125, ((0, 64), (1, 4)))
    value_weight = bell_draw(splits[7], (D, HEADS * HD), D ** -0.5, 0.078125, ((0, 64), (1, 4)))
    return dict(queries=queries, new_keys=new_keys, new_values=new_values, pool=pool, block_table=block_table, block_counts=block_counts, key_weight=key_weight, value_weight=value_weight)


def attend(q_rows, keys, values, live_rows, head_count):
    total = keys.shape[0]
    hist_len = total - q_rows.shape[0]
    scale = 1.0 / math.sqrt(HD)
    q_heads = q_rows.astype(jnp.float32).reshape(q_rows.shape[0], head_count, HD)
    k_heads = keys.astype(jnp.float32).reshape(total, head_count, HD)
    v_heads = values.astype(jnp.float32).reshape(total, head_count, HD)
    scores = jnp.einsum('qhd,khd->hqk', q_heads, k_heads) * scale
    column = jnp.arange(total)[None, :]
    row_pos = jnp.arange(q_rows.shape[0])[:, None]
    allowed = jnp.where(column < hist_len, column < live_rows, column - hist_len <= row_pos)
    scores = jnp.where(allowed[None], scores, -jnp.inf)
    top = lax.optimization_barrier(jnp.max(scores, axis=-1, keepdims=True))
    weights = jnp.exp(scores - top)
    probs = (weights / lax.optimization_barrier(jnp.sum(weights, axis=-1, keepdims=True))).astype(jnp.bfloat16)
    result = jnp.einsum('hqk,khd->qhd', probs.astype(jnp.float32), v_heads)
    return result.reshape(q_rows.shape[0], head_count * HD).astype(jnp.bfloat16)

def reference(queries, new_keys, new_values, pool, block_table, block_counts, key_weight, value_weight):
    table = block_table.reshape(CONV, MAXB)

    def one_conversation(items):
        ids, count, q_rows, k_rows, v_rows = items
        live = (jnp.arange(MAXB) < count).astype(jnp.bfloat16)
        hist = (pool[ids] * live[:, None, None]).reshape(MAXB * BLOCK, D)
        hist_keys = jnp.dot(hist, key_weight, preferred_element_type=jnp.float32).astype(jnp.bfloat16)
        hist_values = jnp.dot(hist, value_weight, preferred_element_type=jnp.float32).astype(jnp.bfloat16)
        keys = jnp.concatenate([hist_keys, k_rows], axis=0)
        values = jnp.concatenate([hist_values, v_rows], axis=0)
        return attend(q_rows, keys, values, count * BLOCK, HEADS)
    return lax.map(one_conversation, (table, block_counts, queries, new_keys, new_values))
```

```python
import functools
import math

import jax
import jax.numpy as jnp
from jax import lax
from jax.experimental import pallas as pl
from jax.experimental.pallas import tpu as pltpu
from jax.sharding import Mesh, PartitionSpec as P

HD = 64
MAXB = 6
USED = 224
GRID = (4, 8, 2)
PLANE = ("y", "z", "core")
BF16 = jnp.bfloat16
F32 = jnp.float32
VMEM_LIMIT = 56 * 1024 * 1024


def dot(a, b, contract=((1,), (0,))):
    return lax.dot_general(a, b, (contract, ((), ())), preferred_element_type=F32)


def iota(shape, dim):
    return lax.broadcasted_iota(jnp.int32, shape, dim)


def live_rows_kernel(counts_ref, table_ref, pool_ref, out_ref):
    convs = counts_ref.shape[1]
    slots = table_ref.shape[1]
    parities, blocks, _ = pool_ref.shape
    used = out_ref.shape[1]
    counts = jnp.broadcast_to(counts_ref[...].astype(F32), (8, convs)).astype(BF16)
    conv_of = iota((convs, slots), 1) // MAXB
    conv_row = iota((convs, slots), 0)
    count_k = dot(counts, (conv_row == conv_of).astype(F32).astype(BF16))[0:1]
    start_k = dot(counts, (conv_row < conv_of).astype(F32).astype(BF16))[0:1]
    slot_k = iota((1, slots), 1) % MAXB
    count_k = count_k.astype(jnp.int32)
    place_k = jnp.where(slot_k < count_k, start_k.astype(jnp.int32) + slot_k, -1)
    takes = (iota((used, slots), 0) == place_k).astype(F32).astype(BF16)
    names = (iota((blocks, slots), 0) == table_ref[...]).astype(F32).astype(BF16)
    pick = dot(takes, names, ((1,), (1,))).astype(BF16)
    for r in range(parities):
        out_ref[r] = dot(pick, pool_ref[r]).astype(BF16)


def live_rows(counts, table, pool):
    blocks, parities, feats = pool.shape
    return pl.pallas_call(
        live_rows_kernel,
        out_shape=jax.ShapeDtypeStruct((parities, USED, feats), BF16),
        in_specs=[pl.BlockSpec(memory_space=pltpu.VMEM)] * 3,
        out_specs=pl.BlockSpec(memory_space=pltpu.VMEM),
        compiler_params=pltpu.CompilerParams(vmem_limit_bytes=VMEM_LIMIT),
        name="live_rows",
    )(counts[None], table[None], jnp.transpose(pool, (1, 0, 2)))


def project_kernel(dims, counts_ref, rows_ref, *rest):
    ny, nz, nh, shard = dims
    first = rest[:nz]
    second = rest[nz : nz + ny]
    out_ref, w_ref, x_ref, acc_ref, acc16_ref, w_sem, x_sem = rest[nz + ny :]
    y, z, core = (lax.axis_index(a) for a in PLANE)
    sign = 1 - 2 * core
    cols = w_ref.shape[1]
    feats = w_ref.shape[0] // nh

    copies = {}
    for s in range(ny):
        plane = lax.rem(y - s * sign + ny, ny)
        for cc in range(2):
            copies[s, "x", cc] = pltpu.make_async_copy(
                rows_ref.at[cc * nh + plane], x_ref.at[2 * s + cc], x_sem.at[2 * s + cc]
            )
        for t in range(nz):
            chip = plane * nz + lax.rem(z - t * sign + nz, nz)
            for k, (src, part, owner) in enumerate(
                ((first[t], s, core), (second[s], t, 1 - core))
            ):
                at = pl.multiple_of((chip * 2 + owner) * shard, shard)
                copies[s, t, k] = pltpu.make_async_copy(
                    src.at[pl.ds(part * shard, shard)],
                    w_ref.at[pl.ds(at, shard)],
                    w_sem.at[(s * nz + t) * 2 + k],
                )
    for c in copies.values():
        c.start()
    half = acc_ref.shape[0] // 2
    tile = 256 if cols % 256 == 0 else cols
    for s in range(ny):
        for key, c in copies.items():
            if key[0] == s:
                c.wait()
        plane = lax.rem(y - s * sign + ny, ny)
        at = pl.multiple_of(plane * feats, feats)

        @pl.loop(0, 2)
        def _(cc):
            @pl.loop(0, cols // tile)
            def _(n):
                lanes = pl.ds(pl.multiple_of(n * tile, tile), tile)
                row = pl.ds(pl.multiple_of(cc * half, half), half)
                part = dot(x_ref[2 * s + cc], w_ref[pl.ds(at, feats), lanes])
                if s == 0:
                    acc_ref[row, lanes] = part
                elif s < ny - 1:
                    acc_ref[row, lanes] += part
                else:
                    acc16_ref[row, lanes] = (acc_ref[row, lanes] + part).astype(BF16)

    convs = counts_ref.shape[1]
    each = out_ref.shape[0] // convs
    chunk = 16 * each
    used = acc_ref.shape[0] // (each // MAXB)

    @pl.loop(0, convs // 16)
    def _(g):
        i = iota((chunk, 1), 0)
        conv = g * 16 + i // each
        inside = i % each
        slot = inside % MAXB
        which = inside // MAXB
        other = iota((chunk, convs), 1)
        counts = counts_ref[...]
        start = jnp.sum(jnp.where(other < conv, counts, 0), axis=1, keepdims=True)
        count = jnp.sum(jnp.where(other == conv, counts, 0), axis=1, keepdims=True)
        source = jnp.where(slot < count, which * used + start + slot, -1)
        put = (iota((chunk, acc_ref.shape[0]), 1) == source).astype(F32).astype(BF16)
        out_ref[pl.ds(pl.multiple_of(g * chunk, chunk), chunk)] = dot(put, acc16_ref[...]).astype(BF16)


def project(counts, rows, first, second, dims):
    ny, nz, nh, shard = dims
    per, feats = rows.shape[1:]
    cols = second[0].shape[1]
    convs = counts.shape[0]
    each = 2 * (per // USED) * MAXB
    hbm = pl.BlockSpec(memory_space=pl.ANY)
    return pl.pallas_call(
        functools.partial(project_kernel, dims),
        out_shape=jax.ShapeDtypeStruct((convs * each, cols), BF16),
        in_specs=[pl.BlockSpec(memory_space=pltpu.VMEM)] + [hbm] * (1 + nz + ny),
        out_specs=pl.BlockSpec(memory_space=pltpu.VMEM),
        scratch_shapes=[
            pltpu.VMEM((nh * feats, cols), BF16),
            pltpu.VMEM((2 * nh, per, feats), BF16),
            pltpu.VMEM((2 * per, cols), F32),
            pltpu.VMEM((2 * per, cols), BF16),
            pltpu.SemaphoreType.DMA((ny * nz * 2,)),
            pltpu.SemaphoreType.DMA((2 * nh,)),
        ],
        compiler_params=pltpu.CompilerParams(vmem_limit_bytes=VMEM_LIMIT),
        cost_estimate=pl.CostEstimate(
            flops=4 * per * nh * feats * cols, bytes_accessed=2 * nh * feats * (cols + 2 * per), transcendentals=0
        ),
        name="project",
    )(counts[None], rows, *first, *second)


def attend_kernel(live_ref, q_ref, k_ref, v_ref, nk_ref, nv_ref, out_ref):
    live = live_ref[0]
    hist = k_ref.shape[0]
    new = nk_ref.shape[0]
    scale = 1.0 / math.sqrt(HD)
    hist_ok = (iota((1, hist), 1) % MAXB) < live
    new_ok = iota((new, new), 1) <= iota((new, new), 0)

    @pl.loop(0, q_ref.shape[1] // (2 * HD))
    def _(pair):
        lanes = pl.ds(pl.multiple_of(pair * 2 * HD, 2 * HD), 2 * HD)
        q, k, v = q_ref[:, lanes], k_ref[:, lanes], v_ref[:, lanes]
        nk, nv = nk_ref[:, lanes], nv_ref[:, lanes]
        low = iota(q.shape, 1) < HD
        outs = []
        for mine in (low, jnp.logical_not(low)):
            qh = jnp.where(mine, q, jnp.zeros_like(q))
            sh = jnp.where(hist_ok, dot(qh, k, ((1,), (1,))) * scale, -jnp.inf)
            sn = jnp.where(new_ok, dot(qh, nk, ((1,), (1,))) * scale, -jnp.inf)
            top = jnp.maximum(
                jnp.max(sh, axis=1, keepdims=True), jnp.max(sn, axis=1, keepdims=True)
            )
            eh, en = jnp.exp(sh - top), jnp.exp(sn - top)
            total = jnp.sum(eh, axis=1, keepdims=True) + jnp.sum(en, axis=1, keepdims=True)
            ph, pn = (eh / total).astype(BF16), (en / total).astype(BF16)
            outs.append(dot(ph, v) + dot(pn, nv))
        out_ref[:, lanes] = jnp.where(low, outs[0], outs[1]).astype(BF16)


def attend(live, q, k, v, nk, nv):
    return pl.pallas_call(
        attend_kernel,
        out_shape=jax.ShapeDtypeStruct(q.shape, BF16),
        in_specs=[pl.BlockSpec(memory_space=pltpu.SMEM)] + [pl.BlockSpec(memory_space=pltpu.VMEM)] * 5,
        out_specs=pl.BlockSpec(memory_space=pltpu.VMEM),
        compiler_params=pltpu.CompilerParams(vmem_limit_bytes=VMEM_LIMIT),
        name="attend",
    )(live, q, k, v, nk, nv)


def ring_step(x, axis):
    n = lax.axis_size(axis)
    perm = []
    for i in range(n):
        perm += [(2 * i, 2 * ((i + 1) % n)), (2 * i + 1, 2 * ((i - 1) % n) + 1)]
    return lax.ppermute(x, (axis, "core"), perm)


def ring(x, axis):
    held = [x]
    for _ in range(lax.axis_size(axis) - 1):
        held.append(ring_step(held[-1], axis))
    return held


def per_device(queries, new_keys, new_values, pool, block_table, block_counts, key_weight, value_weight):
    ny, nz, nh = lax.axis_size("y"), lax.axis_size("z"), lax.axis_size("head")
    core = lax.axis_index("core")
    own = jnp.where(core == 0, key_weight, value_weight)
    away = jnp.where(core == 0, value_weight, key_weight)
    near = lax.ppermute(away, "core", [(0, 1), (1, 0)])

    live = live_rows(block_counts, block_table, pool)
    live = live.reshape(-1, live.shape[2])
    rows = lax.all_gather(live, ("core", "head"), axis=0)

    first = ring(jnp.concatenate(ring(own, "y"), axis=0), "z")
    second = ring(jnp.concatenate(ring(near, "z"), axis=0), "y")
    dims = (ny, nz, nh, key_weight.shape[0])
    sent = project(block_counts, rows, first, second, dims)
    convs = block_counts.shape[0]
    sent = sent.reshape(convs, -1, sent.shape[1])
    got = lax.all_to_all(sent, PLANE, split_axis=0, concat_axis=0, tiled=True)
    got = got.reshape(convs // 2, 2, got.shape[1], got.shape[2])
    keys = got[:, 0].reshape(-1, got.shape[3])
    values = got[:, 1].reshape(-1, got.shape[3])
    mine = lax.axis_index(PLANE)
    count = lax.dynamic_slice(block_counts, (mine,), (1,))
    return attend(count, queries[0], keys, values, new_keys[0], new_values[0])[None]


def solution(mesh):
    grid = Mesh(mesh.devices.reshape(GRID + (mesh.devices.shape[1],)), PLANE + ("head",))
    return jax.shard_map(
        per_device,
        mesh=grid,
        in_specs=(
            P(PLANE, None, "head"),
            P(PLANE, None, "head"),
            P(PLANE, None, "head"),
            P(None, PLANE, "head"),
            P(),
            P(),
            P(PLANE, "head"),
            P(PLANE, "head"),
        ),
        out_specs=P(PLANE, None, "head"),
        check_vma=False,
    )
```

```python
import functools
import math

import jax
import jax.numpy as jnp
from jax import lax
from jax.experimental import pallas as pl
from jax.experimental.pallas import tpu as pltpu
from jax.sharding import Mesh, PartitionSpec as P

HD = 64
MAXB = 6
USED = 224
GRID = (4, 8, 2)
PLANE = ("y", "z", "core")
BF16 = jnp.bfloat16
F32 = jnp.float32
VMEM_LIMIT = 56 * 1024 * 1024


def dot(a, b, contract=((1,), (0,))):
    return lax.dot_general(a, b, (contract, ((), ())), preferred_element_type=F32)


def iota(shape, dim):
    return lax.broadcasted_iota(jnp.int32, shape, dim)


def live_rows_kernel(counts_ref, table_ref, pool_ref, out_ref):
    convs = counts_ref.shape[1]
    slots = table_ref.shape[1]
    parities, blocks, _ = pool_ref.shape
    used = out_ref.shape[1]
    counts = jnp.broadcast_to(counts_ref[...].astype(F32), (8, convs)).astype(BF16)
    conv_of = iota((convs, slots), 1) // MAXB
    conv_row = iota((convs, slots), 0)
    count_k = dot(counts, (conv_row == conv_of).astype(F32).astype(BF16))[0:1]
    start_k = dot(counts, (conv_row < conv_of).astype(F32).astype(BF16))[0:1]
    slot_k = iota((1, slots), 1) % MAXB
    count_k = count_k.astype(jnp.int32)
    place_k = jnp.where(slot_k < count_k, start_k.astype(jnp.int32) + slot_k, -1)
    takes = (iota((used, slots), 0) == place_k).astype(F32).astype(BF16)
    names = (iota((blocks, slots), 0) == table_ref[...]).astype(F32).astype(BF16)
    pick = dot(takes, names, ((1,), (1,))).astype(BF16)
    for r in range(parities):
        out_ref[r] = dot(pick, pool_ref[r]).astype(BF16)


def live_rows(counts, table, pool):
    blocks, parities, feats = pool.shape
    return pl.pallas_call(
        live_rows_kernel,
        out_shape=jax.ShapeDtypeStruct((parities, USED, feats), BF16),
        in_specs=[pl.BlockSpec(memory_space=pltpu.VMEM)] * 3,
        out_specs=pl.BlockSpec(memory_space=pltpu.VMEM),
        compiler_params=pltpu.CompilerParams(vmem_limit_bytes=VMEM_LIMIT),
        name="live_rows",
    )(counts[None], table[None], jnp.transpose(pool, (1, 0, 2)))


def piece_table(ny, nz):
    table = []
    dys = (0, -1, 1, -2)
    dzs = (0, -1, -2, -3, 1, 2, 3, -4)
    for s in range(5):
        for j, dy in enumerate(dys):
            table.append((s, j, dy, -s, 0))
    for s in range(1, 4):
        for j, dy in enumerate(dys):
            table.append((4 + s, j, -dy, s, 0))
    for s in range(3):
        for j, dz in enumerate(dzs):
            table.append((8 + s, j, -s, dz, 1))
    for j, dz in enumerate(dzs):
        table.append((11, j, 1, -dz, 1))
    assert len(table) == ny * nz * 2
    return table


PIECES = 12


def project_kernel(dims, counts_ref, rows_ref, *rest):
    ny, nz, nh, shard = dims
    pieces = rest[:PIECES]
    out_ref, w_ref, x_ref, acc_ref, acc16_ref, w_sem, x_sem = rest[PIECES:]
    y, z, core = (lax.axis_index(a) for a in PLANE)
    sign = 1 - 2 * core
    cols = w_ref.shape[1]
    feats = w_ref.shape[0] // nh

    copies = {}
    for s in range(ny):
        plane = lax.rem(y + s, ny)
        for cc in range(2):
            copies[s, "x", cc] = pltpu.make_async_copy(
                rows_ref.at[cc * nh + plane], x_ref.at[2 * s + cc], x_sem.at[2 * s + cc]
            )
    for k, (src, part, dy, dz, owner) in enumerate(piece_table(ny, nz)):
        chip = lax.rem(y + dy * sign + ny, ny) * nz + lax.rem(z + dz * sign + nz, nz)
        at = pl.multiple_of((chip * 2 + owner) * shard, shard)
        copies[0, "w", k] = pltpu.make_async_copy(
            pieces[src].at[pl.ds(part * shard, shard)],
            w_ref.at[pl.ds(at, shard)],
            w_sem.at[k],
        )
    for c in copies.values():
        c.start()
    half = acc_ref.shape[0] // 2
    tile = 256 if cols % 256 == 0 else cols
    for s in range(ny):
        for key, c in copies.items():
            if key[0] == s:
                c.wait()
        at = pl.multiple_of(lax.rem(y + s, ny) * feats, feats)

        @pl.loop(0, 2)
        def _(cc):
            @pl.loop(0, cols // tile)
            def _(n):
                lanes = pl.ds(pl.multiple_of(n * tile, tile), tile)
                row = pl.ds(pl.multiple_of(cc * half, half), half)
                part = dot(x_ref[2 * s + cc], w_ref[pl.ds(at, feats), lanes])
                if s == 0:
                    acc_ref[row, lanes] = part
                elif s < ny - 1:
                    acc_ref[row, lanes] += part
                else:
                    acc16_ref[row, lanes] = (acc_ref[row, lanes] + part).astype(BF16)

    convs = counts_ref.shape[1]
    each = out_ref.shape[0] // convs
    chunk = 16 * each
    used = acc_ref.shape[0] // (each // MAXB)

    @pl.loop(0, convs // 16)
    def _(g):
        i = iota((chunk, 1), 0)
        conv = g * 16 + i // each
        inside = i % each
        slot = inside % MAXB
        which = inside // MAXB
        other = iota((chunk, convs), 1)
        counts = counts_ref[...]
        start = jnp.sum(jnp.where(other < conv, counts, 0), axis=1, keepdims=True)
        count = jnp.sum(jnp.where(other == conv, counts, 0), axis=1, keepdims=True)
        source = jnp.where(slot < count, which * used + start + slot, -1)
        put = (iota((chunk, acc_ref.shape[0]), 1) == source).astype(F32).astype(BF16)
        out_ref[pl.ds(pl.multiple_of(g * chunk, chunk), chunk)] = dot(put, acc16_ref[...]).astype(BF16)


def project(counts, rows, pieces, dims):
    ny, nz, nh, shard = dims
    per, feats = rows.shape[1:]
    cols = pieces[0].shape[1]
    convs = counts.shape[0]
    each = 2 * (per // USED) * MAXB
    hbm = pl.BlockSpec(memory_space=pl.ANY)
    return pl.pallas_call(
        functools.partial(project_kernel, dims),
        out_shape=jax.ShapeDtypeStruct((convs * each, cols), BF16),
        in_specs=[pl.BlockSpec(memory_space=pltpu.VMEM)] + [hbm] * (1 + PIECES),
        out_specs=pl.BlockSpec(memory_space=pltpu.VMEM),
        scratch_shapes=[
            pltpu.VMEM((nh * feats, cols), BF16),
            pltpu.VMEM((2 * nh, per, feats), BF16),
            pltpu.VMEM((2 * per, cols), F32),
            pltpu.VMEM((2 * per, cols), BF16),
            pltpu.SemaphoreType.DMA((ny * nz * 2,)),
            pltpu.SemaphoreType.DMA((2 * nh,)),
        ],
        compiler_params=pltpu.CompilerParams(vmem_limit_bytes=VMEM_LIMIT),
        cost_estimate=pl.CostEstimate(
            flops=4 * per * nh * feats * cols, bytes_accessed=2 * nh * feats * (cols + 2 * per), transcendentals=0
        ),
        name="project",
    )(counts[None], rows, *pieces)


def attend_kernel(live_ref, q_ref, k_ref, v_ref, nk_ref, nv_ref, out_ref):
    live = live_ref[0]
    hist = k_ref.shape[0]
    new = nk_ref.shape[0]
    scale = 1.0 / math.sqrt(HD)
    hist_ok = (iota((1, hist), 1) % MAXB) < live
    new_ok = iota((new, new), 1) <= iota((new, new), 0)

    @pl.loop(0, q_ref.shape[1] // (2 * HD))
    def _(pair):
        lanes = pl.ds(pl.multiple_of(pair * 2 * HD, 2 * HD), 2 * HD)
        q, k, v = q_ref[:, lanes], k_ref[:, lanes], v_ref[:, lanes]
        nk, nv = nk_ref[:, lanes], nv_ref[:, lanes]
        low = iota(q.shape, 1) < HD
        outs = []
        for mine in (low, jnp.logical_not(low)):
            qh = jnp.where(mine, q, jnp.zeros_like(q))
            sh = jnp.where(hist_ok, dot(qh, k, ((1,), (1,))) * scale, -jnp.inf)
            sn = jnp.where(new_ok, dot(qh, nk, ((1,), (1,))) * scale, -jnp.inf)
            top = jnp.maximum(
                jnp.max(sh, axis=1, keepdims=True), jnp.max(sn, axis=1, keepdims=True)
            )
            eh, en = jnp.exp(sh - top), jnp.exp(sn - top)
            total = jnp.sum(eh, axis=1, keepdims=True) + jnp.sum(en, axis=1, keepdims=True)
            ph, pn = (eh / total).astype(BF16), (en / total).astype(BF16)
            outs.append(dot(ph, v) + dot(pn, nv))
        out_ref[:, lanes] = jnp.where(low, outs[0], outs[1]).astype(BF16)


def attend(live, q, k, v, nk, nv):
    return pl.pallas_call(
        attend_kernel,
        out_shape=jax.ShapeDtypeStruct(q.shape, BF16),
        in_specs=[pl.BlockSpec(memory_space=pltpu.SMEM)] + [pl.BlockSpec(memory_space=pltpu.VMEM)] * 5,
        out_specs=pl.BlockSpec(memory_space=pltpu.VMEM),
        compiler_params=pltpu.CompilerParams(vmem_limit_bytes=VMEM_LIMIT),
        name="attend",
    )(live, q, k, v, nk, nv)


def ring_step(x, axis):
    n = lax.axis_size(axis)
    perm = []
    for i in range(n):
        perm += [(2 * i, 2 * ((i + 1) % n)), (2 * i + 1, 2 * ((i - 1) % n) + 1)]
    return lax.ppermute(x, (axis, "core"), perm)


def swap_cores(x):
    return lax.ppermute(x, "core", [(0, 1), (1, 0)])


def kinds(x):
    half = x.shape[0] // 2
    return x[:half], x[half:]


def gather_weights(key_weight, value_weight):
    upper = lax.axis_index("core") == 0
    mine = jnp.where(upper, key_weight, value_weight)
    other = jnp.where(upper, value_weight, key_weight)
    own = jnp.concatenate([mine, other])
    near = swap_cores(jnp.concatenate([other, mine]))
    zero = jnp.where(upper, own, near)
    one = jnp.where(upper, near, own)

    y1 = ring_step(zero, "y")
    y2 = ring_step(kinds(y1)[0], "y")
    got = swap_cores(jnp.concatenate([y1, y2]))
    n = key_weight.shape[0]
    group = jnp.concatenate(
        [
            kinds(zero)[0], kinds(y1)[0], got[n : 2 * n], y2,
            kinds(zero)[1], kinds(y1)[1], got[:n], got[2 * n :],
        ]
    )
    z1 = ring_step(group, "z")
    z2 = ring_step(z1, "z")
    z3 = ring_step(z2, "z")
    z4 = ring_step(kinds(z3)[0], "z")
    across = [swap_cores(kinds(t)[1]) for t in (z1, z2, z3)]
    first = [group, z1, z2, z3, z4] + across

    r1 = ring_step(one, "z")
    r2 = ring_step(r1, "z")
    r3 = ring_step(r2, "z")
    r4 = ring_step(kinds(r3)[0], "z")
    ring = [one, r1, r2, r3]
    got = swap_cores(jnp.concatenate([r1, r2, r3, r4]))
    line = jnp.concatenate(
        [kinds(t)[0] for t in ring]
        + [got[(2 * k + 1) * n : (2 * k + 2) * n] for k in range(3)]
        + [r4]
        + [kinds(t)[1] for t in ring]
        + [got[2 * k * n : (2 * k + 1) * n] for k in range(3)]
        + [got[6 * n :]]
    )
    l1 = ring_step(line, "y")
    l2 = ring_step(kinds(l1)[0], "y")
    second = [line, l1, l2, swap_cores(kinds(l1)[1])]
    return first + second


def per_device(queries, new_keys, new_values, pool, block_table, block_counts, key_weight, value_weight):
    ny, nz, nh = lax.axis_size("y"), lax.axis_size("z"), lax.axis_size("head")
    live = live_rows(block_counts, block_table, pool)
    live = live.reshape(-1, live.shape[2])
    rows = lax.all_gather(live, ("core", "head"), axis=0)

    pieces = gather_weights(key_weight, value_weight)
    dims = (ny, nz, nh, key_weight.shape[0])
    sent = project(block_counts, rows, pieces, dims)
    convs = block_counts.shape[0]
    sent = sent.reshape(convs, -1, sent.shape[1])
    got = lax.all_to_all(sent, PLANE, split_axis=0, concat_axis=0, tiled=True)
    got = got.reshape(convs // 2, 2, got.shape[1], got.shape[2])
    keys = got[:, 0].reshape(-1, got.shape[3])
    values = got[:, 1].reshape(-1, got.shape[3])
    mine = lax.axis_index(PLANE)
    count = lax.dynamic_slice(block_counts, (mine,), (1,))
    return attend(count, queries[0], keys, values, new_keys[0], new_values[0])[None]


def solution(mesh):
    grid = Mesh(mesh.devices.reshape(GRID + (mesh.devices.shape[1],)), PLANE + ("head",))
    return jax.shard_map(
        per_device,
        mesh=grid,
        in_specs=(
            P(PLANE, None, "head"),
            P(PLANE, None, "head"),
            P(PLANE, None, "head"),
            P(None, PLANE, "head"),
            P(),
            P(),
            P(PLANE, "head"),
            P(PLANE, "head"),
        ),
        out_specs=P(PLANE, None, "head"),
        check_vma=False,
    )
```

```python
import functools
import math

import jax
import jax.numpy as jnp
from jax import lax
from jax.experimental import pallas as pl
from jax.experimental.pallas import tpu as pltpu
from jax.sharding import Mesh, PartitionSpec as P

HD = 64
MAXB = 6
USED = 224
GRID = (4, 8, 2)
PLANE = ("y", "z", "core")
BF16 = jnp.bfloat16
F32 = jnp.float32
VMEM_LIMIT = 56 * 1024 * 1024


def dot(a, b, contract=((1,), (0,))):
    return lax.dot_general(a, b, (contract, ((), ())), preferred_element_type=F32)


def iota(shape, dim):
    return lax.broadcasted_iota(jnp.int32, shape, dim)


def live_rows_kernel(counts_ref, table_ref, pool_ref, out_ref):
    convs = counts_ref.shape[1]
    slots = table_ref.shape[1]
    parities, blocks, _ = pool_ref.shape
    used = out_ref.shape[1]
    counts = jnp.broadcast_to(counts_ref[...].astype(F32), (8, convs)).astype(BF16)
    conv_of = iota((convs, slots), 1) // MAXB
    conv_row = iota((convs, slots), 0)
    count_k = dot(counts, (conv_row == conv_of).astype(F32).astype(BF16))[0:1]
    start_k = dot(counts, (conv_row < conv_of).astype(F32).astype(BF16))[0:1]
    slot_k = iota((1, slots), 1) % MAXB
    count_k = count_k.astype(jnp.int32)
    place_k = jnp.where(slot_k < count_k, start_k.astype(jnp.int32) + slot_k, -1)
    takes = (iota((used, slots), 0) == place_k).astype(F32).astype(BF16)
    names = (iota((blocks, slots), 0) == table_ref[...]).astype(F32).astype(BF16)
    pick = dot(takes, names, ((1,), (1,))).astype(BF16)
    for r in range(parities):
        out_ref[r] = dot(pick, pool_ref[r]).astype(BF16)


def live_rows(counts, table, pool):
    blocks, parities, feats = pool.shape
    return pl.pallas_call(
        live_rows_kernel,
        out_shape=jax.ShapeDtypeStruct((parities, USED, feats), BF16),
        in_specs=[pl.BlockSpec(memory_space=pltpu.VMEM)] * 3,
        out_specs=pl.BlockSpec(memory_space=pltpu.VMEM),
        compiler_params=pltpu.CompilerParams(vmem_limit_bytes=VMEM_LIMIT),
        name="live_rows",
    )(counts[None], table[None], jnp.transpose(pool, (1, 0, 2)))


def piece_table(ny, nz):
    table = []
    dys = (0, -1, 1, -2)
    dzs = (0, -1, -2, -3, 1, 2, 3, -4)
    for s in range(5):
        for j, dy in enumerate(dys):
            table.append((s, j, dy, -s, 0))
    for s in range(1, 4):
        for j, dy in enumerate(dys):
            table.append((4 + s, j, -dy, s, 0))
    for s in range(3):
        for j, dz in enumerate(dzs):
            table.append((8 + s, j, -s, dz, 1))
    for j, dz in enumerate(dzs):
        table.append((11, j, 1, -dz, 1))
    assert len(table) == ny * nz * 2
    return table


PIECES = 12


def project_kernel(dims, counts_ref, *rest):
    ny, nz, nh, shard = dims
    rows = rest[: 2 * nh]
    pieces = rest[2 * nh : 2 * nh + PIECES]
    out_ref, w_ref, x_ref, put_ref, acc_ref, acc16_ref, w_sem, x_sem = rest[2 * nh + PIECES :]
    y, z, core = (lax.axis_index(a) for a in PLANE)
    head = lax.axis_index("head")
    sign = 1 - 2 * core
    cols = w_ref.shape[1]
    feats = w_ref.shape[0] // nh

    w_copies, x_copies = [], []
    for k, (src, part, dy, dz, owner) in enumerate(piece_table(ny, nz)):
        chip = lax.rem(y + dy * sign + ny, ny) * nz + lax.rem(z + dz * sign + nz, nz)
        at = pl.multiple_of((chip * 2 + owner) * shard, shard)
        w_copies.append(
            pltpu.make_async_copy(
                pieces[src].at[pl.ds(part * shard, shard)],
                w_ref.at[pl.ds(at, shard)],
                w_sem.at[k],
            )
        )
    for k in range(2 * nh):
        who = core if k % 2 == 0 else 1 - core
        x_copies.append(
            pltpu.make_async_copy(rows[k], x_ref.at[2 * (k // 2) + who], x_sem.at[k])
        )
    for c in w_copies + x_copies:
        c.start()

    convs = counts_ref.shape[1]
    each = out_ref.shape[0] // convs
    chunk = 16 * each
    total = acc_ref.shape[0]
    used = total // (each // MAXB)

    @pl.loop(0, convs // 16)
    def _(g):
        i = iota((chunk, 1), 0) + g * chunk
        conv = lax.shift_right_logical(i * (65536 // each + 1), 16)
        inside = i - conv * each
        which = lax.shift_right_logical(inside * (65536 // MAXB + 1), 16)
        slot = inside - which * MAXB
        other = iota((chunk, convs), 1)
        counts = counts_ref[...]
        both = jnp.sum(
            jnp.where(other < conv, counts * 8, jnp.where(other == conv, counts, 0)),
            axis=1,
            keepdims=True,
        )
        start, count = lax.shift_right_logical(both, 3), lax.bitwise_and(both, 7)
        source = jnp.where(slot < count, which * used + start + slot, -1)
        rows_of = pl.ds(pl.multiple_of(g * chunk, chunk), chunk)
        put_ref[rows_of] = (iota((chunk, total), 1) == source).astype(F32).astype(BF16)

    for c in w_copies:
        c.wait()
    half = total // 2
    quarters = (0, -1, 1, -2)
    for s in range(nh):
        for c in x_copies[2 * s : 2 * s + 2]:
            c.wait()
        quarter = lax.rem(head + quarters[s] * sign + nh, nh)
        at = pl.multiple_of(quarter * feats, feats)

        @pl.loop(0, 2)
        def _(cc):
            row = pl.ds(pl.multiple_of(cc * half, half), half)
            part = dot(x_ref[2 * s + cc], w_ref[pl.ds(at, feats)])
            if s == 0:
                acc_ref[row] = part
            elif s < nh - 1:
                acc_ref[row] += part
            else:
                acc16_ref[row] = (acc_ref[row] + part).astype(BF16)

    @pl.loop(0, convs // 16)
    def _(g):
        rows_of = pl.ds(pl.multiple_of(g * chunk, chunk), chunk)
        out_ref[rows_of] = dot(put_ref[rows_of], acc16_ref[...]).astype(BF16)


def project(counts, rows, pieces, dims):
    ny, nz, nh, shard = dims
    per, feats = rows[0].shape
    cols = pieces[0].shape[1]
    convs = counts.shape[0]
    each = 2 * (per // USED) * MAXB
    hbm = pl.BlockSpec(memory_space=pl.ANY)
    return pl.pallas_call(
        functools.partial(project_kernel, dims),
        out_shape=jax.ShapeDtypeStruct((convs * each, cols), BF16),
        in_specs=[pl.BlockSpec(memory_space=pltpu.VMEM)] + [hbm] * (2 * nh + PIECES),
        out_specs=pl.BlockSpec(memory_space=pltpu.VMEM),
        scratch_shapes=[
            pltpu.VMEM((nh * feats, cols), BF16),
            pltpu.VMEM((2 * nh, per, feats), BF16),
            pltpu.VMEM((convs * each, 2 * per), BF16),
            pltpu.VMEM((2 * per, cols), F32),
            pltpu.VMEM((2 * per, cols), BF16),
            pltpu.SemaphoreType.DMA((ny * nz * 2,)),
            pltpu.SemaphoreType.DMA((2 * nh,)),
        ],
        compiler_params=pltpu.CompilerParams(vmem_limit_bytes=VMEM_LIMIT),
        cost_estimate=pl.CostEstimate(
            flops=4 * per * nh * feats * cols, bytes_accessed=2 * nh * feats * (cols + 2 * per), transcendentals=0
        ),
        name="project",
    )(counts[None], *rows, *pieces)


def attend_kernel(live_ref, q_ref, k_ref, v_ref, nk_ref, nv_ref, out_ref):
    live = live_ref[0]
    hist = k_ref.shape[0]
    new = nk_ref.shape[0]
    scale = 1.0 / math.sqrt(HD)
    hist_ok = (iota((1, hist), 1) % MAXB) < live
    new_ok = iota((new, new), 1) <= iota((new, new), 0)

    @pl.loop(0, q_ref.shape[1] // (2 * HD))
    def _(pair):
        lanes = pl.ds(pl.multiple_of(pair * 2 * HD, 2 * HD), 2 * HD)
        q = q_ref[:, lanes] * jnp.asarray(scale, BF16)
        k, v = k_ref[:, lanes], v_ref[:, lanes]
        nk, nv = nk_ref[:, lanes], nv_ref[:, lanes]
        low = iota(q.shape, 1) < HD
        outs = []
        for mine in (low, jnp.logical_not(low)):
            qh = jnp.where(mine, q, jnp.zeros_like(q))
            sh = jnp.where(hist_ok, dot(qh, k, ((1,), (1,))), -jnp.inf)
            sn = jnp.where(new_ok, dot(qh, nk, ((1,), (1,))), -jnp.inf)
            top = jnp.maximum(
                jnp.max(sh, axis=1, keepdims=True), jnp.max(sn, axis=1, keepdims=True)
            )
            eh, en = jnp.exp(sh - top), jnp.exp(sn - top)
            total = jnp.sum(eh, axis=1, keepdims=True) + jnp.sum(en, axis=1, keepdims=True)
            share = 1.0 / total
            ph, pn = (eh * share).astype(BF16), (en * share).astype(BF16)
            outs.append(dot(ph, v) + dot(pn, nv))
        out_ref[:, lanes] = jnp.where(low, outs[0], outs[1]).astype(BF16)


def attend(live, q, k, v, nk, nv):
    return pl.pallas_call(
        attend_kernel,
        out_shape=jax.ShapeDtypeStruct(q.shape, BF16),
        in_specs=[pl.BlockSpec(memory_space=pltpu.SMEM)] + [pl.BlockSpec(memory_space=pltpu.VMEM)] * 5,
        out_specs=pl.BlockSpec(memory_space=pltpu.VMEM),
        compiler_params=pltpu.CompilerParams(vmem_limit_bytes=VMEM_LIMIT),
        name="attend",
    )(live, q, k, v, nk, nv)


def ring_step(x, axis, way=1):
    n = lax.axis_size(axis)
    order = (axis, "core") if axis != "head" else ("core", axis)
    place = (lambda i, c: 2 * i + c) if axis != "head" else (lambda i, c: c * n + i)
    perm = []
    for i in range(n):
        perm += [(place(i, 0), place((i + way) % n, 0)), (place(i, 1), place((i - way) % n, 1))]
    return lax.ppermute(x, order, perm)


def gather_rows(own):
    behind = ring_step(own, "head")
    ahead = ring_step(own, "head", -1)
    opposite = ring_step(behind, "head")
    return [
        own, swap_cores(own),
        behind, swap_cores(ahead),
        ahead, swap_cores(behind),
        opposite, swap_cores(opposite),
    ]


def swap_cores(x):
    return lax.ppermute(x, "core", [(0, 1), (1, 0)])


def kinds(x):
    half = x.shape[0] // 2
    return x[:half], x[half:]


def gather_weights(key_weight, value_weight):
    upper = lax.axis_index("core") == 0
    mine = jnp.where(upper, key_weight, value_weight)
    other = jnp.where(upper, value_weight, key_weight)
    own = jnp.concatenate([mine, other])
    near = swap_cores(jnp.concatenate([other, mine]))
    zero = jnp.where(upper, own, near)
    one = jnp.where(upper, near, own)

    y1 = ring_step(zero, "y")
    y2 = ring_step(kinds(y1)[0], "y")
    got = swap_cores(jnp.concatenate([y1, y2]))
    n = key_weight.shape[0]
    group = jnp.concatenate(
        [
            kinds(zero)[0], kinds(y1)[0], got[n : 2 * n], y2,
            kinds(zero)[1], kinds(y1)[1], got[:n], got[2 * n :],
        ]
    )
    z1 = ring_step(group, "z")
    z2 = ring_step(z1, "z")
    z3 = ring_step(z2, "z")
    z4 = ring_step(kinds(z3)[0], "z")
    across = [swap_cores(kinds(t)[1]) for t in (z1, z2, z3)]
    first = [group, z1, z2, z3, z4] + across

    r1 = ring_step(one, "z")
    r2 = ring_step(r1, "z")
    r3 = ring_step(r2, "z")
    r4 = ring_step(kinds(r3)[0], "z")
    ring = [one, r1, r2, r3]
    got = swap_cores(jnp.concatenate([r1, r2, r3, r4]))
    line = jnp.concatenate(
        [kinds(t)[0] for t in ring]
        + [got[(2 * k + 1) * n : (2 * k + 2) * n] for k in range(3)]
        + [r4]
        + [kinds(t)[1] for t in ring]
        + [got[2 * k * n : (2 * k + 1) * n] for k in range(3)]
        + [got[6 * n :]]
    )
    l1 = ring_step(line, "y")
    l2 = ring_step(kinds(l1)[0], "y")
    second = [line, l1, l2, swap_cores(kinds(l1)[1])]
    return first + second


def per_device(queries, new_keys, new_values, pool, block_table, block_counts, key_weight, value_weight):
    ny, nz, nh = lax.axis_size("y"), lax.axis_size("z"), lax.axis_size("head")
    live = live_rows(block_counts, block_table, pool)
    live = live.reshape(-1, live.shape[2])
    rows = gather_rows(live)

    pieces = gather_weights(key_weight, value_weight)
    dims = (ny, nz, nh, key_weight.shape[0])
    sent = project(block_counts, rows, pieces, dims)
    convs = block_counts.shape[0]
    sent = sent.reshape(convs, -1, sent.shape[1])
    got = lax.all_to_all(sent, PLANE, split_axis=0, concat_axis=0, tiled=True)
    got = got.reshape(convs // 2, 2, got.shape[1], got.shape[2])
    keys = got[:, 0].reshape(-1, got.shape[3])
    values = got[:, 1].reshape(-1, got.shape[3])
    mine = lax.axis_index(PLANE)
    count = lax.dynamic_slice(block_counts, (mine,), (1,))
    return attend(count, queries[0], keys, values, new_keys[0], new_values[0])[None]


def solution(mesh):
    grid = Mesh(mesh.devices.reshape(GRID + (mesh.devices.shape[1],)), PLANE + ("head",))
    return jax.shard_map(
        per_device,
        mesh=grid,
        in_specs=(
            P(PLANE, None, "head"),
            P(PLANE, None, "head"),
            P(PLANE, None, "head"),
            P(None, PLANE, "head"),
            P(),
            P(),
            P(PLANE, "head"),
            P(PLANE, "head"),
        ),
        out_specs=P(PLANE, None, "head"),
        check_vma=False,
    )
```

```python
import functools
import math

import jax
import jax.numpy as jnp
from jax import lax
from jax.experimental import pallas as pl
from jax.experimental.pallas import tpu as pltpu
from jax.sharding import Mesh, PartitionSpec as P

HD = 64
MAXB = 6
USED = 224
GRID = (4, 8, 2)
PLANE = ("y", "z", "core")
BF16 = jnp.bfloat16
F32 = jnp.float32
VMEM_LIMIT = 56 * 1024 * 1024


def dot(a, b, contract=((1,), (0,))):
    return lax.dot_general(a, b, (contract, ((), ())), preferred_element_type=F32)


def iota(shape, dim):
    return lax.broadcasted_iota(jnp.int32, shape, dim)


def live_rows_kernel(counts_ref, table_ref, pool_ref, out_ref):
    convs = counts_ref.shape[1]
    slots = table_ref.shape[1]
    parities, blocks, _ = pool_ref.shape
    used = out_ref.shape[1]
    counts = jnp.broadcast_to(counts_ref[...].astype(F32), (8, convs)).astype(BF16)
    conv_of = iota((convs, slots), 1) // MAXB
    conv_row = iota((convs, slots), 0)
    count_k = dot(counts, (conv_row == conv_of).astype(F32).astype(BF16))[0:1]
    start_k = dot(counts, (conv_row < conv_of).astype(F32).astype(BF16))[0:1]
    slot_k = iota((1, slots), 1) % MAXB
    count_k = count_k.astype(jnp.int32)
    place_k = jnp.where(slot_k < count_k, start_k.astype(jnp.int32) + slot_k, -1)
    takes = (iota((used, slots), 0) == place_k).astype(F32).astype(BF16)
    names = (iota((blocks, slots), 0) == table_ref[...]).astype(F32).astype(BF16)
    pick = dot(takes, names, ((1,), (1,))).astype(BF16)
    for r in range(parities):
        out_ref[r] = dot(pick, pool_ref[r]).astype(BF16)


def live_rows(counts, table, pool):
    blocks, parities, feats = pool.shape
    return pl.pallas_call(
        live_rows_kernel,
        out_shape=jax.ShapeDtypeStruct((parities, USED, feats), BF16),
        in_specs=[pl.BlockSpec(memory_space=pltpu.VMEM)] * 3,
        out_specs=pl.BlockSpec(memory_space=pltpu.VMEM),
        compiler_params=pltpu.CompilerParams(vmem_limit_bytes=VMEM_LIMIT),
        name="live_rows",
    )(counts[None], table[None], jnp.transpose(pool, (1, 0, 2)))


def piece_table(ny, nz):
    assert (ny, nz) == (4, 8)
    dys = (0, -1, 1, -2)
    table = [(s, j, dy, -s) for s in range(5) for j, dy in enumerate(dys)]
    return table + [(4 + s, j, -dy, s) for s in range(1, 4) for j, dy in enumerate(dys)]


def project_kernel(dims, counts_ref, *rest):
    ny, nz, nh, shard = dims
    rows = rest[: 2 * nh]
    pieces = rest[2 * nh : -8]
    out_ref, w_ref, x_ref, put_ref, acc_ref, acc16_ref, w_sem, x_sem = rest[-8:]
    y, z, core = (lax.axis_index(a) for a in PLANE)
    head = lax.axis_index("head")
    sign = 1 - 2 * core
    cols = w_ref.shape[1]
    feats = w_ref.shape[0] // nh

    w_copies, x_copies = [], []
    if len(pieces) == 1:
        for k in range(nh):
            part = pl.ds(k * feats, feats)
            w_copies.append(pltpu.make_async_copy(pieces[0].at[part], w_ref.at[part], w_sem.at[k]))
    else:
        for k, (src, part, dy, dz) in enumerate(piece_table(ny, nz)):
            chip = lax.rem(y + dy * sign + ny, ny) * nz + lax.rem(z + dz * sign + nz, nz)
            at = pl.multiple_of(chip * shard, shard)
            w_copies.append(
                pltpu.make_async_copy(
                    pieces[src].at[pl.ds(part * shard, shard)],
                    w_ref.at[pl.ds(at, shard)],
                    w_sem.at[k],
                )
            )
    for k in range(2 * nh):
        who = core if k % 2 == 0 else 1 - core
        x_copies.append(
            pltpu.make_async_copy(rows[k], x_ref.at[2 * (k // 2) + who], x_sem.at[k])
        )
    for c in w_copies + x_copies:
        c.start()

    convs = counts_ref.shape[1]
    each = out_ref.shape[0] // convs
    chunk = 16 * each
    total = acc_ref.shape[0]
    used = total // (each // MAXB)

    @pl.loop(0, convs // 16)
    def _(g):
        i = iota((chunk, 1), 0) + g * chunk
        conv = lax.shift_right_logical(i * (65536 // each + 1), 16)
        inside = i - conv * each
        which = lax.shift_right_logical(inside * (65536 // MAXB + 1), 16)
        slot = inside - which * MAXB
        other = iota((chunk, convs), 1)
        counts = counts_ref[...]
        both = jnp.sum(
            jnp.where(other < conv, counts * 8, jnp.where(other == conv, counts, 0)),
            axis=1,
            keepdims=True,
        )
        start, count = lax.shift_right_logical(both, 3), lax.bitwise_and(both, 7)
        source = jnp.where(slot < count, which * used + start + slot, -1)
        rows_of = pl.ds(pl.multiple_of(g * chunk, chunk), chunk)
        put_ref[rows_of] = (iota((chunk, total), 1) == source).astype(F32).astype(BF16)

    for c in w_copies:
        c.wait()
    half = total // 2
    quarters = (0, -1, 1, -2)
    for s in range(nh):
        for c in x_copies[2 * s : 2 * s + 2]:
            c.wait()
        quarter = lax.rem(head + quarters[s] * sign + nh, nh)
        at = pl.multiple_of(quarter * feats, feats)

        @pl.loop(0, 2)
        def _(cc):
            row = pl.ds(pl.multiple_of(cc * half, half), half)
            part = dot(x_ref[2 * s + cc], w_ref[pl.ds(at, feats)])
            if s == 0:
                acc_ref[row] = part
            elif s < nh - 1:
                acc_ref[row] += part
            else:
                acc16_ref[row] = (acc_ref[row] + part).astype(BF16)

    @pl.loop(0, convs // 16)
    def _(g):
        rows_of = pl.ds(pl.multiple_of(g * chunk, chunk), chunk)
        out_ref[rows_of] = dot(put_ref[rows_of], acc16_ref[...]).astype(BF16)


def project(counts, rows, pieces, dims):
    ny, nz, nh, shard = dims
    per, feats = rows[0].shape
    cols = pieces[0].shape[1]
    convs = counts.shape[0]
    each = 2 * (per // USED) * MAXB
    hbm = pl.BlockSpec(memory_space=pl.ANY)
    return pl.pallas_call(
        functools.partial(project_kernel, dims),
        out_shape=jax.ShapeDtypeStruct((convs * each, cols), BF16),
        in_specs=[pl.BlockSpec(memory_space=pltpu.VMEM)] + [hbm] * (2 * nh + len(pieces)),
        out_specs=pl.BlockSpec(memory_space=pltpu.VMEM),
        scratch_shapes=[
            pltpu.VMEM((nh * feats, cols), BF16),
            pltpu.VMEM((2 * nh, per, feats), BF16),
            pltpu.VMEM((convs * each, 2 * per), BF16),
            pltpu.VMEM((2 * per, cols), F32),
            pltpu.VMEM((2 * per, cols), BF16),
            pltpu.SemaphoreType.DMA((ny * nz,)),
            pltpu.SemaphoreType.DMA((2 * nh,)),
        ],
        compiler_params=pltpu.CompilerParams(vmem_limit_bytes=VMEM_LIMIT),
        cost_estimate=pl.CostEstimate(
            flops=4 * per * nh * feats * cols, bytes_accessed=2 * nh * feats * (cols + 2 * per), transcendentals=0
        ),
        name="project",
    )(counts[None], *rows, *pieces)


def attend_kernel(first, live_ref, q_ref, k_ref, v_ref, nk_ref, nv_ref, *rest):
    out_ref = rest[-1]
    if first:
        out_ref[:, :first] = rest[0][...]
    live = live_ref[0]
    hist = k_ref.shape[0]
    new = nk_ref.shape[0]
    scale = 1.0 / math.sqrt(HD)
    hist_ok = (iota((1, hist), 1) % MAXB) < live
    token = iota((2 * new, new), 0)
    token = jnp.where(token < new, token, token - new)
    new_ok = iota((2 * new, new), 1) <= token

    @pl.loop(0, k_ref.shape[1] // (2 * HD))
    def _(pair):
        lanes = pl.ds(pl.multiple_of(pair * 2 * HD, 2 * HD), 2 * HD)
        all_lanes = pl.ds(pl.multiple_of(first + pair * 2 * HD, 2 * HD), 2 * HD)
        q = q_ref[:, all_lanes] * jnp.asarray(scale, BF16)
        k, v = k_ref[:, lanes], v_ref[:, lanes]
        nk, nv = nk_ref[:, all_lanes], nv_ref[:, all_lanes]
        low = iota(q.shape, 1) < HD
        none = jnp.zeros_like(q)
        q2 = jnp.concatenate([jnp.where(low, q, none), jnp.where(low, none, q)], axis=0)
        sh = jnp.where(hist_ok, dot(q2, k, ((1,), (1,))), -jnp.inf)
        sn = jnp.where(new_ok, dot(q2, nk, ((1,), (1,))), -jnp.inf)
        top = jnp.maximum(
            jnp.max(sh, axis=1, keepdims=True), jnp.max(sn, axis=1, keepdims=True)
        )
        eh, en = jnp.exp(sh - top), jnp.exp(sn - top)
        total = jnp.sum(eh, axis=1, keepdims=True) + jnp.sum(en, axis=1, keepdims=True)
        share = 1.0 / total
        ph, pn = (eh * share).astype(BF16), (en * share).astype(BF16)
        out = dot(ph, v) + dot(pn, nv)
        out_ref[:, all_lanes] = jnp.where(low, out[:new], out[new:]).astype(BF16)


def attend(live, q, k, v, nk, nv, before=None):
    first = 0 if before is None else before.shape[1]
    more = () if before is None else (before,)
    return pl.pallas_call(
        functools.partial(attend_kernel, first),
        out_shape=jax.ShapeDtypeStruct((q.shape[0], first + k.shape[1]), BF16),
        in_specs=[pl.BlockSpec(memory_space=pltpu.SMEM)]
        + [pl.BlockSpec(memory_space=pltpu.VMEM)] * (5 + len(more)),
        out_specs=pl.BlockSpec(memory_space=pltpu.VMEM),
        compiler_params=pltpu.CompilerParams(vmem_limit_bytes=VMEM_LIMIT),
        name="attend",
    )(live, q, k, v, nk, nv, *more)


def ring_step(x, axis, way=1):
    n = lax.axis_size(axis)
    order = (axis, "core") if axis != "head" else ("core", axis)
    place = (lambda i, c: 2 * i + c) if axis != "head" else (lambda i, c: c * n + i)
    perm = []
    for i in range(n):
        perm += [(place(i, 0), place((i + way) % n, 0)), (place(i, 1), place((i - way) % n, 1))]
    return lax.ppermute(x, order, perm)


def gather_rows(own):
    behind = ring_step(own, "head")
    ahead = ring_step(own, "head", -1)
    opposite = ring_step(behind, "head")
    return [
        own, swap_cores(own),
        behind, swap_cores(ahead),
        ahead, swap_cores(behind),
        opposite, swap_cores(opposite),
    ]


def swap_cores(x):
    return lax.ppermute(x, "core", [(0, 1), (1, 0)])


def kinds(x):
    half = x.shape[0] // 2
    return x[:half], x[half:]


def gather_weights(key_weight, value_weight):
    upper = lax.axis_index("core") == 0
    half = key_weight.shape[1] // 2
    mine = jnp.where(upper, key_weight, value_weight)
    other = jnp.where(upper, value_weight, key_weight)
    n = mine.shape[0]
    near = swap_cores(jnp.concatenate([other, mine]))

    def chip(a, b):
        return jnp.where(upper, jnp.concatenate([a, b]), jnp.concatenate([b, a]))

    chip_mine = chip(mine, near[:n])
    second = lax.all_gather(chip_mine[:, half:], ("y", "z"), axis=0, tiled=True)

    n = 2 * n
    own = jnp.concatenate([chip_mine[:, :half], chip(other, near[n // 2 :])[:, :half]])
    y1 = ring_step(own, "y")
    y2 = ring_step(kinds(y1)[0], "y")
    got = swap_cores(jnp.concatenate([y1, y2]))
    group = jnp.concatenate(
        [own[:n], y1[:n], got[n : 2 * n], y2, own[n:], y1[n:], got[:n], got[2 * n :]]
    )
    z1 = ring_step(group, "z")
    z2 = ring_step(z1, "z")
    z3 = ring_step(z2, "z")
    z4 = ring_step(kinds(z3)[0], "z")
    across = [swap_cores(kinds(t)[1]) for t in (z1, z2, z3)]
    return [group, z1, z2, z3, z4] + across, [second]


def per_device(queries, new_keys, new_values, pool, block_table, block_counts, key_weight, value_weight):
    ny, nz, nh = lax.axis_size("y"), lax.axis_size("z"), lax.axis_size("head")
    live = live_rows(block_counts, block_table, pool)
    live = live.reshape(-1, live.shape[2])
    rows = gather_rows(live)

    halves = gather_weights(key_weight, value_weight)
    dims = (ny, nz, nh, 2 * key_weight.shape[0])
    convs = block_counts.shape[0]
    count = lax.dynamic_slice(block_counts, (lax.axis_index(PLANE),), (1,))
    out = None
    for pieces in halves:
        sent = project(block_counts, rows, pieces, dims)
        sent = sent.reshape(convs, -1, sent.shape[1])
        got = lax.all_to_all(sent, PLANE, split_axis=0, concat_axis=0, tiled=True)
        got = got.reshape(convs // 2, 2, got.shape[1], got.shape[2])
        keys = got[:, 0].reshape(-1, got.shape[3])
        values = got[:, 1].reshape(-1, got.shape[3])
        out = attend(count, queries[0], keys, values, new_keys[0], new_values[0], out)
    return out[None]


def solution(mesh):
    grid = Mesh(mesh.devices.reshape(GRID + (mesh.devices.shape[1],)), PLANE + ("head",))
    return jax.shard_map(
        per_device,
        mesh=grid,
        in_specs=(
            P(PLANE, None, "head"),
            P(PLANE, None, "head"),
            P(PLANE, None, "head"),
            P(None, PLANE, "head"),
            P(),
            P(),
            P(PLANE, "head"),
            P(PLANE, "head"),
        ),
        out_specs=P(PLANE, None, "head"),
        check_vma=False,
    )
```

```python
import functools
import math

import jax
import jax.numpy as jnp
from jax import lax
from jax.experimental import pallas as pl
from jax.experimental.pallas import tpu as pltpu
from jax.sharding import Mesh, PartitionSpec as P

HD = 64
MAXB = 6
USED = 224
FIRST = 256
GRID = (4, 8, 2)
PLANE = ("y", "z", "core")
BF16 = jnp.bfloat16
F32 = jnp.float32
VMEM_LIMIT = 56 * 1024 * 1024


def dot(a, b, contract=((1,), (0,))):
    return lax.dot_general(a, b, (contract, ((), ())), preferred_element_type=F32)


def iota(shape, dim):
    return lax.broadcasted_iota(jnp.int32, shape, dim)


def live_rows_kernel(counts_ref, table_ref, pool_ref, out_ref):
    convs = counts_ref.shape[1]
    slots = table_ref.shape[1]
    parities, blocks, _ = pool_ref.shape
    used = out_ref.shape[1]
    counts = jnp.broadcast_to(counts_ref[...].astype(F32), (8, convs)).astype(BF16)
    conv_of = iota((convs, slots), 1) // MAXB
    conv_row = iota((convs, slots), 0)
    count_k = dot(counts, (conv_row == conv_of).astype(F32).astype(BF16))[0:1]
    start_k = dot(counts, (conv_row < conv_of).astype(F32).astype(BF16))[0:1]
    slot_k = iota((1, slots), 1) % MAXB
    count_k = count_k.astype(jnp.int32)
    place_k = jnp.where(slot_k < count_k, start_k.astype(jnp.int32) + slot_k, -1)
    takes = (iota((used, slots), 0) == place_k).astype(F32).astype(BF16)
    names = (iota((blocks, slots), 0) == table_ref[...]).astype(F32).astype(BF16)
    pick = dot(takes, names, ((1,), (1,))).astype(BF16)
    for r in range(parities):
        out_ref[r] = dot(pick, pool_ref[r]).astype(BF16)


def live_rows(counts, table, pool):
    blocks, parities, feats = pool.shape
    return pl.pallas_call(
        live_rows_kernel,
        out_shape=jax.ShapeDtypeStruct((parities, USED, feats), BF16),
        in_specs=[pl.BlockSpec(memory_space=pltpu.VMEM)] * 3,
        out_specs=pl.BlockSpec(memory_space=pltpu.VMEM),
        compiler_params=pltpu.CompilerParams(vmem_limit_bytes=VMEM_LIMIT),
        name="live_rows",
    )(counts[None], table[None], jnp.transpose(pool, (1, 0, 2)))


def piece_table(ny, nz):
    assert (ny, nz) == (4, 8)
    dys = (0, -1, 1, -2)
    table = [(s, j, dy, -s) for s in range(5) for j, dy in enumerate(dys)]
    return table + [(4 + s, j, -dy, s) for s in range(1, 4) for j, dy in enumerate(dys)]


def project_kernel(dims, counts_ref, *rest):
    ny, nz, nh, shard = dims
    rows = rest[: 2 * nh]
    pieces = rest[2 * nh : -8]
    out_ref, w_ref, x_ref, put_ref, acc_ref, acc16_ref, w_sem, x_sem = rest[-8:]
    y, z, core = (lax.axis_index(a) for a in PLANE)
    head = lax.axis_index("head")
    sign = 1 - 2 * core
    cols = w_ref.shape[1]
    feats = w_ref.shape[0] // nh

    w_copies, x_copies = [], []
    if len(pieces) == 1:
        for k in range(nh):
            part = pl.ds(k * feats, feats)
            w_copies.append(pltpu.make_async_copy(pieces[0].at[part], w_ref.at[part], w_sem.at[k]))
    else:
        for k, (src, part, dy, dz) in enumerate(piece_table(ny, nz)):
            chip = lax.rem(y + dy * sign + ny, ny) * nz + lax.rem(z + dz * sign + nz, nz)
            at = pl.multiple_of(chip * shard, shard)
            w_copies.append(
                pltpu.make_async_copy(
                    pieces[src].at[pl.ds(part * shard, shard)],
                    w_ref.at[pl.ds(at, shard)],
                    w_sem.at[k],
                )
            )
    for k in range(2 * nh):
        who = core if k % 2 == 0 else 1 - core
        x_copies.append(
            pltpu.make_async_copy(rows[k], x_ref.at[2 * (k // 2) + who], x_sem.at[k])
        )
    for c in w_copies + x_copies[:2]:
        c.start()

    convs = counts_ref.shape[1]
    each = out_ref.shape[0] // convs
    chunk = 16 * each
    total = acc_ref.shape[0]
    used = total // (each // MAXB)

    @pl.loop(0, convs // 16)
    def _(g):
        i = iota((chunk, 1), 0) + g * chunk
        conv = lax.shift_right_logical(i * (65536 // each + 1), 16)
        inside = i - conv * each
        which = lax.shift_right_logical(inside * (65536 // MAXB + 1), 16)
        slot = inside - which * MAXB
        other = iota((chunk, convs), 1)
        counts = counts_ref[...]
        both = jnp.sum(
            jnp.where(other < conv, counts * 8, jnp.where(other == conv, counts, 0)),
            axis=1,
            keepdims=True,
        )
        start, count = lax.shift_right_logical(both, 3), lax.bitwise_and(both, 7)
        source = jnp.where(slot < count, which * used + start + slot, -1)
        rows_of = pl.ds(pl.multiple_of(g * chunk, chunk), chunk)
        put_ref[rows_of] = (iota((chunk, total), 1) == source).astype(F32).astype(BF16)

    for c in w_copies:
        c.wait()
    half = total // 2
    quarters = (0, -1, 1, -2)
    for s in range(nh):
        for c in x_copies[2 * s : 2 * s + 2]:
            c.wait()
        for c in x_copies[2 * s + 2 : 2 * s + 4]:
            c.start()
        quarter = lax.rem(head + quarters[s] * sign + nh, nh)
        at = pl.multiple_of(quarter * feats, feats)

        @pl.loop(0, 2)
        def _(cc):
            row = pl.ds(pl.multiple_of(cc * half, half), half)
            part = dot(x_ref[2 * s + cc], w_ref[pl.ds(at, feats)])
            if s == 0:
                acc_ref[row] = part
            elif s < nh - 1:
                acc_ref[row] += part
            else:
                acc16_ref[row] = (acc_ref[row] + part).astype(BF16)

    @pl.loop(0, convs // 16)
    def _(g):
        rows_of = pl.ds(pl.multiple_of(g * chunk, chunk), chunk)
        out_ref[rows_of] = dot(put_ref[rows_of], acc16_ref[...]).astype(BF16)


def project(counts, rows, pieces, dims):
    ny, nz, nh, shard = dims
    per, feats = rows[0].shape
    cols = pieces[0].shape[1]
    convs = counts.shape[0]
    each = 2 * (per // USED) * MAXB
    hbm = pl.BlockSpec(memory_space=pl.ANY)
    return pl.pallas_call(
        functools.partial(project_kernel, dims),
        out_shape=jax.ShapeDtypeStruct((convs * each, cols), BF16),
        in_specs=[pl.BlockSpec(memory_space=pltpu.VMEM)] + [hbm] * (2 * nh + len(pieces)),
        out_specs=pl.BlockSpec(memory_space=pltpu.VMEM),
        scratch_shapes=[
            pltpu.VMEM((nh * feats, cols), BF16),
            pltpu.VMEM((2 * nh, per, feats), BF16),
            pltpu.VMEM((convs * each, 2 * per), BF16),
            pltpu.VMEM((2 * per, cols), F32),
            pltpu.VMEM((2 * per, cols), BF16),
            pltpu.SemaphoreType.DMA((ny * nz,)),
            pltpu.SemaphoreType.DMA((2 * nh,)),
        ],
        compiler_params=pltpu.CompilerParams(vmem_limit_bytes=VMEM_LIMIT),
        cost_estimate=pl.CostEstimate(
            flops=4 * per * nh * feats * cols, bytes_accessed=2 * nh * feats * (cols + 2 * per), transcendentals=0
        ),
        name="project",
    )(counts[None], *rows, *pieces)


def attend_kernel(first, live_ref, q_ref, k_ref, v_ref, nk_ref, nv_ref, *rest):
    out_ref = rest[-1]
    if first:
        out_ref[:, :first] = rest[0][...]
    live = live_ref[0]
    hist = k_ref.shape[0]
    new = nk_ref.shape[0]
    scale = 1.0 / math.sqrt(HD)
    hist_ok = (iota((1, hist), 1) % MAXB) < live
    token = iota((2 * new, new), 0)
    token = jnp.where(token < new, token, token - new)
    new_ok = iota((2 * new, new), 1) <= token

    @pl.loop(0, k_ref.shape[1] // (2 * HD))
    def _(pair):
        lanes = pl.ds(pl.multiple_of(pair * 2 * HD, 2 * HD), 2 * HD)
        all_lanes = pl.ds(pl.multiple_of(first + pair * 2 * HD, 2 * HD), 2 * HD)
        q = q_ref[:, all_lanes] * jnp.asarray(scale, BF16)
        k, v = k_ref[:, lanes], v_ref[:, lanes]
        nk, nv = nk_ref[:, all_lanes], nv_ref[:, all_lanes]
        low = iota(q.shape, 1) < HD
        none = jnp.zeros_like(q)
        q2 = jnp.concatenate([jnp.where(low, q, none), jnp.where(low, none, q)], axis=0)
        sh = jnp.where(hist_ok, dot(q2, k, ((1,), (1,))), -jnp.inf)
        sn = jnp.where(new_ok, dot(q2, nk, ((1,), (1,))), -jnp.inf)
        top = jnp.maximum(
            jnp.max(sh, axis=1, keepdims=True), jnp.max(sn, axis=1, keepdims=True)
        )
        eh, en = jnp.exp(sh - top), jnp.exp(sn - top)
        total = jnp.sum(eh, axis=1, keepdims=True) + jnp.sum(en, axis=1, keepdims=True)
        share = 1.0 / total
        ph, pn = (eh * share).astype(BF16), (en * share).astype(BF16)
        out = dot(ph, v) + dot(pn, nv)
        out_ref[:, all_lanes] = jnp.where(low, out[:new], out[new:]).astype(BF16)


def attend(live, q, k, v, nk, nv, before=None):
    first = 0 if before is None else before.shape[1]
    more = () if before is None else (before,)
    return pl.pallas_call(
        functools.partial(attend_kernel, first),
        out_shape=jax.ShapeDtypeStruct((q.shape[0], first + k.shape[1]), BF16),
        in_specs=[pl.BlockSpec(memory_space=pltpu.SMEM)]
        + [pl.BlockSpec(memory_space=pltpu.VMEM)] * (5 + len(more)),
        out_specs=pl.BlockSpec(memory_space=pltpu.VMEM),
        compiler_params=pltpu.CompilerParams(vmem_limit_bytes=VMEM_LIMIT),
        name="attend",
    )(live, q, k, v, nk, nv, *more)


def ring_step(x, axis, way=1):
    n = lax.axis_size(axis)
    order = (axis, "core") if axis != "head" else ("core", axis)
    place = (lambda i, c: 2 * i + c) if axis != "head" else (lambda i, c: c * n + i)
    perm = []
    for i in range(n):
        perm += [(place(i, 0), place((i + way) % n, 0)), (place(i, 1), place((i - way) % n, 1))]
    return lax.ppermute(x, order, perm)


def swap_cores(x):
    return lax.ppermute(x, "core", [(0, 1), (1, 0)])


def kinds(x):
    half = x.shape[0] // 2
    return x[:half], x[half:]


def gather(key_weight, value_weight, rows_of):
    hold = lax.optimization_barrier
    upper = lax.axis_index("core") == 0
    mine = jnp.where(upper, key_weight, value_weight)
    other = jnp.where(upper, value_weight, key_weight)
    n = mine.shape[0]
    both, rows = hold((jnp.concatenate([other, mine]), rows_of()))
    near = swap_cores(both)

    def chip(a, b):
        return jnp.where(upper, jnp.concatenate([a, b]), jnp.concatenate([b, a]))

    chip_mine = chip(mine, near[:n])
    second = lax.all_gather(chip_mine[:, FIRST:], ("y", "z"), axis=0, tiled=True)

    n = 2 * n
    own = jnp.concatenate([chip_mine[:, :FIRST], chip(other, near[n // 2 :])[:, :FIRST]])
    behind = ring_step(rows, "head")
    ahead = ring_step(rows, "head", -1)
    y1 = ring_step(own, "y")
    y2 = ring_step(kinds(y1)[0], "y")
    got = swap_cores(jnp.concatenate([y1, y2]))
    group = jnp.concatenate(
        [own[:n], y1[:n], got[n : 2 * n], y2, own[n:], y1[n:], got[:n], got[2 * n :]]
    )
    z1 = ring_step(group, "z")
    z2 = ring_step(z1, "z")
    z2, z1 = hold((z2, z1))
    z3 = ring_step(z2, "z")
    opposite = ring_step(behind, "head")
    across = [swap_cores(kinds(z1)[1])]
    near_rows = [swap_cores(rows), swap_cores(ahead), swap_cores(behind)]
    z3, z2, opposite = hold((z3, z2, opposite))
    z4 = ring_step(kinds(z3)[0], "z")
    across += [swap_cores(kinds(z2)[1]), swap_cores(kinds(z3)[1])]
    near_rows.append(swap_cores(opposite))
    rows = [r for pair in zip((rows, behind, ahead, opposite), near_rows) for r in pair]
    return rows, ([group, z1, z2, z3, z4] + across, [second])


def per_device(queries, new_keys, new_values, pool, block_table, block_counts, key_weight, value_weight):
    ny, nz, nh = lax.axis_size("y"), lax.axis_size("z"), lax.axis_size("head")
    def rows_of():
        live = live_rows(block_counts, block_table, pool)
        return live.reshape(-1, live.shape[2])

    rows, parts = gather(key_weight, value_weight, rows_of)
    dims = (ny, nz, nh, 2 * key_weight.shape[0])
    convs = block_counts.shape[0]
    count = lax.dynamic_slice(block_counts, (lax.axis_index(PLANE),), (1,))
    out = None
    for pieces in parts:
        sent = project(block_counts, rows, pieces, dims)
        sent = sent.reshape(convs, -1, sent.shape[1])
        got = lax.all_to_all(sent, PLANE, split_axis=0, concat_axis=0, tiled=True)
        got = got.reshape(convs // 2, 2, got.shape[1], got.shape[2])
        keys = got[:, 0].reshape(-1, got.shape[3])
        values = got[:, 1].reshape(-1, got.shape[3])
        out = attend(count, queries[0], keys, values, new_keys[0], new_values[0], out)
    return out[None]


def solution(mesh):
    grid = Mesh(mesh.devices.reshape(GRID + (mesh.devices.shape[1],)), PLANE + ("head",))
    return jax.shard_map(
        per_device,
        mesh=grid,
        in_specs=(
            P(PLANE, None, "head"),
            P(PLANE, None, "head"),
            P(PLANE, None, "head"),
            P(None, PLANE, "head"),
            P(),
            P(),
            P(PLANE, "head"),
            P(PLANE, "head"),
        ),
        out_specs=P(PLANE, None, "head"),
        check_vma=False,
    )
```

```python
import functools
import math

import jax
import jax.numpy as jnp
from jax import lax
from jax.experimental import pallas as pl
from jax.experimental.pallas import tpu as pltpu
from jax.sharding import Mesh, PartitionSpec as P

HD = 64
MAXB = 6
USED = 224
FIRST = 384
GRID = (4, 8, 2)
PLANE = ("y", "z", "core")
BF16 = jnp.bfloat16
F32 = jnp.float32
VMEM_LIMIT = 56 * 1024 * 1024


def dot(a, b, contract=((1,), (0,))):
    return lax.dot_general(a, b, (contract, ((), ())), preferred_element_type=F32)


def iota(shape, dim):
    return lax.broadcasted_iota(jnp.int32, shape, dim)


def live_rows_kernel(counts_ref, table_ref, pool_ref, out_ref):
    convs = counts_ref.shape[1]
    slots = table_ref.shape[1]
    parities, blocks, _ = pool_ref.shape
    used = out_ref.shape[1]
    counts = jnp.broadcast_to(counts_ref[...].astype(F32), (8, convs)).astype(BF16)
    conv_of = iota((convs, slots), 1) // MAXB
    conv_row = iota((convs, slots), 0)
    count_k = dot(counts, (conv_row == conv_of).astype(F32).astype(BF16))[0:1]
    start_k = dot(counts, (conv_row < conv_of).astype(F32).astype(BF16))[0:1]
    slot_k = iota((1, slots), 1) % MAXB
    count_k = count_k.astype(jnp.int32)
    place_k = jnp.where(slot_k < count_k, start_k.astype(jnp.int32) + slot_k, -1)
    takes = (iota((used, slots), 0) == place_k).astype(F32).astype(BF16)
    names = (iota((blocks, slots), 0) == table_ref[...]).astype(F32).astype(BF16)
    pick = dot(takes, names, ((1,), (1,))).astype(BF16)
    for r in range(parities):
        out_ref[r] = dot(pick, pool_ref[r]).astype(BF16)


def live_rows(counts, table, pool):
    blocks, parities, feats = pool.shape
    return pl.pallas_call(
        live_rows_kernel,
        out_shape=jax.ShapeDtypeStruct((parities, USED, feats), BF16),
        in_specs=[pl.BlockSpec(memory_space=pltpu.VMEM)] * 3,
        out_specs=pl.BlockSpec(memory_space=pltpu.VMEM),
        compiler_params=pltpu.CompilerParams(vmem_limit_bytes=VMEM_LIMIT),
        name="live_rows",
    )(counts[None], table[None], jnp.transpose(pool, (1, 0, 2)))


def piece_table(ny, nz, part):
    assert (ny, nz) == (4, 8)
    dys = (0, -1, 1, -2)
    dzs = (0, -1, -2, -3, 1, 2, 3, -4)
    if part == 0:
        table = [(s, j, dy, -s) for s in range(5) for j, dy in enumerate(dys)]
        return table + [(4 + s, j, -dy, s) for s in range(1, 4) for j, dy in enumerate(dys)]
    table = [(s, j, -s, dz) for s in range(3) for j, dz in enumerate(dzs)]
    return table + [(3, j, 1, -dz) for j, dz in enumerate(dzs)]


def project_kernel(dims, counts_ref, *rest):
    ny, nz, nh, shard = dims
    rows = rest[: 2 * nh]
    pieces = rest[2 * nh : -8]
    out_ref, w_ref, x_ref, put_ref, acc_ref, acc16_ref, w_sem, x_sem = rest[-8:]
    y, z, core = (lax.axis_index(a) for a in PLANE)
    head = lax.axis_index("head")
    sign = 1 - 2 * core
    cols = w_ref.shape[1]
    feats = w_ref.shape[0] // nh

    w_copies, x_copies = [], []
    for k, (src, part, dy, dz) in enumerate(piece_table(ny, nz, 0 if len(pieces) == nz else 1)):
        chip = lax.rem(y + dy * sign + ny, ny) * nz + lax.rem(z + dz * sign + nz, nz)
        at = pl.multiple_of(chip * shard, shard)
        w_copies.append(
            pltpu.make_async_copy(
                pieces[src].at[pl.ds(part * shard, shard)],
                w_ref.at[pl.ds(at, shard)],
                w_sem.at[k],
            )
        )
    for k in range(2 * nh):
        who = core if k % 2 == 0 else 1 - core
        x_copies.append(
            pltpu.make_async_copy(rows[k], x_ref.at[2 * (k // 2) + who], x_sem.at[k])
        )
    for c in w_copies + x_copies[:2]:
        c.start()

    convs = counts_ref.shape[1]
    each = out_ref.shape[0] // convs
    chunk = 16 * each
    total = acc_ref.shape[0]
    used = total // (each // MAXB)

    @pl.loop(0, convs // 16)
    def _(g):
        i = iota((chunk, 1), 0) + g * chunk
        conv = lax.shift_right_logical(i * (65536 // each + 1), 16)
        inside = i - conv * each
        which = lax.shift_right_logical(inside * (65536 // MAXB + 1), 16)
        slot = inside - which * MAXB
        other = iota((chunk, convs), 1)
        counts = counts_ref[...]
        both = jnp.sum(
            jnp.where(other < conv, counts * 8, jnp.where(other == conv, counts, 0)),
            axis=1,
            keepdims=True,
        )
        start, count = lax.shift_right_logical(both, 3), lax.bitwise_and(both, 7)
        source = jnp.where(slot < count, which * used + start + slot, -1)
        rows_of = pl.ds(pl.multiple_of(g * chunk, chunk), chunk)
        put_ref[rows_of] = (iota((chunk, total), 1) == source).astype(F32).astype(BF16)

    for c in w_copies:
        c.wait()
    half = total // 2
    quarters = (0, -1, 1, -2)
    for s in range(nh):
        for c in x_copies[2 * s : 2 * s + 2]:
            c.wait()
        for c in x_copies[2 * s + 2 : 2 * s + 4]:
            c.start()
        quarter = lax.rem(head + quarters[s] * sign + nh, nh)
        at = pl.multiple_of(quarter * feats, feats)

        @pl.loop(0, 2)
        def _(cc):
            row = pl.ds(pl.multiple_of(cc * half, half), half)
            part = dot(x_ref[2 * s + cc], w_ref[pl.ds(at, feats)])
            if s == 0:
                acc_ref[row] = part
            elif s < nh - 1:
                acc_ref[row] += part
            else:
                acc16_ref[row] = (acc_ref[row] + part).astype(BF16)

    @pl.loop(0, convs // 16)
    def _(g):
        rows_of = pl.ds(pl.multiple_of(g * chunk, chunk), chunk)
        out_ref[rows_of] = dot(put_ref[rows_of], acc16_ref[...]).astype(BF16)


def project(counts, rows, pieces, dims):
    ny, nz, nh, shard = dims
    per, feats = rows[0].shape
    cols = pieces[0].shape[1]
    convs = counts.shape[0]
    each = 2 * (per // USED) * MAXB
    hbm = pl.BlockSpec(memory_space=pl.ANY)
    return pl.pallas_call(
        functools.partial(project_kernel, dims),
        out_shape=jax.ShapeDtypeStruct((convs * each, cols), BF16),
        in_specs=[pl.BlockSpec(memory_space=pltpu.VMEM)] + [hbm] * (2 * nh + len(pieces)),
        out_specs=pl.BlockSpec(memory_space=pltpu.VMEM),
        scratch_shapes=[
            pltpu.VMEM((nh * feats, cols), BF16),
            pltpu.VMEM((2 * nh, per, feats), BF16),
            pltpu.VMEM((convs * each, 2 * per), BF16),
            pltpu.VMEM((2 * per, cols), F32),
            pltpu.VMEM((2 * per, cols), BF16),
            pltpu.SemaphoreType.DMA((ny * nz,)),
            pltpu.SemaphoreType.DMA((2 * nh,)),
        ],
        compiler_params=pltpu.CompilerParams(vmem_limit_bytes=VMEM_LIMIT),
        cost_estimate=pl.CostEstimate(
            flops=4 * per * nh * feats * cols, bytes_accessed=2 * nh * feats * (cols + 2 * per), transcendentals=0
        ),
        name="project",
    )(counts[None], *rows, *pieces)


def attend_kernel(first, live_ref, q_ref, k_ref, v_ref, nk_ref, nv_ref, *rest):
    out_ref = rest[-1]
    if first:
        out_ref[:, :first] = rest[0][...]
    live = live_ref[0]
    hist = k_ref.shape[0]
    new = nk_ref.shape[0]
    scale = 1.0 / math.sqrt(HD)
    hist_ok = (iota((1, hist), 1) % MAXB) < live
    token = iota((2 * new, new), 0)
    token = jnp.where(token < new, token, token - new)
    new_ok = iota((2 * new, new), 1) <= token

    @pl.loop(0, k_ref.shape[1] // (2 * HD))
    def _(pair):
        lanes = pl.ds(pl.multiple_of(pair * 2 * HD, 2 * HD), 2 * HD)
        all_lanes = pl.ds(pl.multiple_of(first + pair * 2 * HD, 2 * HD), 2 * HD)
        q = q_ref[:, all_lanes] * jnp.asarray(scale, BF16)
        k, v = k_ref[:, lanes], v_ref[:, lanes]
        nk, nv = nk_ref[:, all_lanes], nv_ref[:, all_lanes]
        low = iota(q.shape, 1) < HD
        none = jnp.zeros_like(q)
        q2 = jnp.concatenate([jnp.where(low, q, none), jnp.where(low, none, q)], axis=0)
        sh = jnp.where(hist_ok, dot(q2, k, ((1,), (1,))), -jnp.inf)
        sn = jnp.where(new_ok, dot(q2, nk, ((1,), (1,))), -jnp.inf)
        top = jnp.maximum(
            jnp.max(sh, axis=1, keepdims=True), jnp.max(sn, axis=1, keepdims=True)
        )
        eh, en = jnp.exp(sh - top), jnp.exp(sn - top)
        total = jnp.sum(eh, axis=1, keepdims=True) + jnp.sum(en, axis=1, keepdims=True)
        share = 1.0 / total
        ph, pn = (eh * share).astype(BF16), (en * share).astype(BF16)
        out = dot(ph, v) + dot(pn, nv)
        out_ref[:, all_lanes] = jnp.where(low, out[:new], out[new:]).astype(BF16)


def attend(live, q, k, v, nk, nv, before=None):
    first = 0 if before is None else before.shape[1]
    more = () if before is None else (before,)
    return pl.pallas_call(
        functools.partial(attend_kernel, first),
        out_shape=jax.ShapeDtypeStruct((q.shape[0], first + k.shape[1]), BF16),
        in_specs=[pl.BlockSpec(memory_space=pltpu.SMEM)]
        + [pl.BlockSpec(memory_space=pltpu.VMEM)] * (5 + len(more)),
        out_specs=pl.BlockSpec(memory_space=pltpu.VMEM),
        compiler_params=pltpu.CompilerParams(vmem_limit_bytes=VMEM_LIMIT),
        name="attend",
    )(live, q, k, v, nk, nv, *more)


def ring_step(x, axis, way=1):
    n = lax.axis_size(axis)
    order = (axis, "core") if axis != "head" else ("core", axis)
    place = (lambda i, c: 2 * i + c) if axis != "head" else (lambda i, c: c * n + i)
    perm = []
    for i in range(n):
        perm += [(place(i, 0), place((i + way) % n, 0)), (place(i, 1), place((i - way) % n, 1))]
    return lax.ppermute(x, order, perm)


def swap_cores(x):
    return lax.ppermute(x, "core", [(0, 1), (1, 0)])


def kinds(x):
    half = x.shape[0] // 2
    return x[:half], x[half:]


hold = lax.optimization_barrier


def gather(key_weight, value_weight, rows_of):
    upper = lax.axis_index("core") == 0
    mine = jnp.where(upper, key_weight, value_weight)
    other = jnp.where(upper, value_weight, key_weight)
    n = mine.shape[0]
    both, rows = hold((jnp.concatenate([other, mine]), rows_of()))
    near = swap_cores(both)

    def chip(a, b):
        return jnp.where(upper, jnp.concatenate([a, b]), jnp.concatenate([b, a]))

    chip_mine = chip(mine, near[:n])
    chip_other = chip(other, near[n:])
    n = 2 * n
    own = jnp.concatenate([chip_mine[:, :FIRST], chip_other[:, :FIRST]])
    own_b = jnp.concatenate([chip_mine[:, FIRST:], chip_other[:, FIRST:]])
    behind = ring_step(rows, "head")
    ahead = ring_step(rows, "head", -1)
    y1 = ring_step(own, "y")
    y2 = ring_step(kinds(y1)[0], "y")
    got = swap_cores(jnp.concatenate([y1, y2]))
    group = jnp.concatenate(
        [own[:n], y1[:n], got[n : 2 * n], y2, own[n:], y1[n:], got[:n], got[2 * n :]]
    )
    r1 = ring_step(own_b, "z")
    r2 = ring_step(r1, "z")
    m = group.shape[0]
    z1 = ring_step(jnp.concatenate([group, r2]), "z")
    r3 = z1[m:]
    z2 = ring_step(z1[: m + n], "z")
    z2, behind, ahead = hold((z2, behind, ahead))
    r4 = z2[m:]
    got = swap_cores(jnp.concatenate([r1, r2, r3, r4]))
    ring = [own_b, r1, r2, r3]
    line = jnp.concatenate(
        [t[:n] for t in ring]
        + [got[(2 * k + 1) * n : (2 * k + 2) * n] for k in range(3)]
        + [r4]
        + [t[n:] for t in ring]
        + [got[2 * k * n : (2 * k + 1) * n] for k in range(3)]
        + [got[6 * n :]]
    )
    z3 = ring_step(z2[:m], "z")
    opposite = ring_step(behind, "head")
    l1 = ring_step(line, "y")
    z4 = ring_step(z3[: m // 2], "z")
    near_rows = [swap_cores(t) for t in (rows, ahead, behind, opposite)]
    across = [swap_cores(t[m // 2 : m]) for t in (z1, z2, z3)]
    rows = [r for pair in zip((rows, behind, ahead, opposite), near_rows) for r in pair]
    return rows, [group, z1, z2, z3, z4] + across, (line, l1)


def per_device(queries, new_keys, new_values, pool, block_table, block_counts, key_weight, value_weight):
    ny, nz, nh = lax.axis_size("y"), lax.axis_size("z"), lax.axis_size("head")
    def rows_of():
        live = live_rows(block_counts, block_table, pool)
        return live.reshape(-1, live.shape[2])

    rows, first, (line, l1) = gather(key_weight, value_weight, rows_of)
    dims = (ny, nz, nh, 2 * key_weight.shape[0])
    convs = block_counts.shape[0]
    count = lax.dynamic_slice(block_counts, (lax.axis_index(PLANE),), (1,))

    def move(sent):
        sent = sent.reshape(convs, -1, sent.shape[1])
        got = lax.all_to_all(sent, PLANE, split_axis=0, concat_axis=0, tiled=True)
        got = got.reshape(convs // 2, 2, got.shape[1], got.shape[2])
        return got[:, 0].reshape(-1, got.shape[3]), got[:, 1].reshape(-1, got.shape[3])

    sent = project(block_counts, rows, first, dims)
    _, l1 = hold((sent, l1))
    keys, values = move(sent)
    l2 = ring_step(kinds(l1)[0], "y")
    second = [line, l1, l2, swap_cores(kinds(l1)[1])]
    out = attend(count, queries[0], keys, values, new_keys[0], new_values[0])
    keys, values = move(project(block_counts, rows, second, dims))
    return attend(count, queries[0], keys, values, new_keys[0], new_values[0], out)[None]


def solution(mesh):
    grid = Mesh(mesh.devices.reshape(GRID + (mesh.devices.shape[1],)), PLANE + ("head",))
    return jax.shard_map(
        per_device,
        mesh=grid,
        in_specs=(
            P(PLANE, None, "head"),
            P(PLANE, None, "head"),
            P(PLANE, None, "head"),
            P(None, PLANE, "head"),
            P(),
            P(),
            P(PLANE, "head"),
            P(PLANE, "head"),
        ),
        out_specs=P(PLANE, None, "head"),
        check_vma=False,
    )
```

```python
import functools
import math

import jax
import jax.numpy as jnp
from jax import lax
from jax.experimental import pallas as pl
from jax.experimental.pallas import tpu as pltpu
from jax.sharding import Mesh, PartitionSpec as P

HD = 64
MAXB = 6
USED = 224
GRID = (4, 8, 2)
PLANE = ("y", "z", "core")
BF16 = jnp.bfloat16
F32 = jnp.float32
VMEM_LIMIT = 56 * 1024 * 1024


def dot(a, b, contract=((1,), (0,))):
    return lax.dot_general(a, b, (contract, ((), ())), preferred_element_type=F32)


def iota(shape, dim):
    return lax.broadcasted_iota(jnp.int32, shape, dim)


def live_rows_kernel(counts_ref, table_ref, pool_ref, out_ref):
    convs = counts_ref.shape[1]
    slots = table_ref.shape[1]
    parities, blocks, _ = pool_ref.shape
    used = out_ref.shape[1]
    counts = jnp.broadcast_to(counts_ref[...].astype(F32), (8, convs)).astype(BF16)
    conv_of = iota((convs, slots), 1) // MAXB
    conv_row = iota((convs, slots), 0)
    count_k = dot(counts, (conv_row == conv_of).astype(F32).astype(BF16))[0:1]
    start_k = dot(counts, (conv_row < conv_of).astype(F32).astype(BF16))[0:1]
    slot_k = iota((1, slots), 1) % MAXB
    count_k = count_k.astype(jnp.int32)
    place_k = jnp.where(slot_k < count_k, start_k.astype(jnp.int32) + slot_k, -1)
    takes = (iota((used, slots), 0) == place_k).astype(F32).astype(BF16)
    names = (iota((blocks, slots), 0) == table_ref[...]).astype(F32).astype(BF16)
    pick = dot(takes, names, ((1,), (1,))).astype(BF16)
    for r in range(parities):
        out_ref[r] = dot(pick, pool_ref[r]).astype(BF16)


def live_rows(counts, table, pool):
    blocks, parities, feats = pool.shape
    return pl.pallas_call(
        live_rows_kernel,
        out_shape=jax.ShapeDtypeStruct((parities, USED, feats), BF16),
        in_specs=[pl.BlockSpec(memory_space=pltpu.VMEM)] * 3,
        out_specs=pl.BlockSpec(memory_space=pltpu.VMEM),
        compiler_params=pltpu.CompilerParams(vmem_limit_bytes=VMEM_LIMIT),
        name="live_rows",
    )(counts[None], table[None], jnp.transpose(pool, (1, 0, 2)))


def piece_table(ny, nz):
    table = []
    dys = (0, -1, 1, -2)
    dzs = (0, -1, -2, -3, 1, 2, 3, -4)
    for s in range(5):
        for j, dy in enumerate(dys):
            table.append((s, j, dy, -s, 0))
    for s in range(1, 4):
        for j, dy in enumerate(dys):
            table.append((4 + s, j, -dy, s, 0))
    for s in range(3):
        for j, dz in enumerate(dzs):
            table.append((8 + s, j, -s, dz, 1))
    for j, dz in enumerate(dzs):
        table.append((11, j, 1, -dz, 1))
    assert len(table) == ny * nz * 2
    return table


PIECES = 12


def project_kernel(dims, counts_ref, *rest):
    ny, nz, nh, shard = dims
    rows = rest[: 2 * nh]
    pieces = rest[2 * nh : 2 * nh + PIECES]
    out_ref, w_ref, x_ref, put_ref, acc_ref, acc16_ref, w_sem, x_sem = rest[2 * nh + PIECES :]
    y, z, core = (lax.axis_index(a) for a in PLANE)
    head = lax.axis_index("head")
    sign = 1 - 2 * core
    cols = w_ref.shape[1]
    feats = w_ref.shape[0] // nh

    w_copies, x_copies = [], []
    for k, (src, part, dy, dz, owner) in enumerate(piece_table(ny, nz)):
        chip = lax.rem(y + dy * sign + ny, ny) * nz + lax.rem(z + dz * sign + nz, nz)
        at = pl.multiple_of((chip * 2 + owner) * shard, shard)
        w_copies.append(
            pltpu.make_async_copy(
                pieces[src].at[pl.ds(part * shard, shard)],
                w_ref.at[pl.ds(at, shard)],
                w_sem.at[k],
            )
        )
    for k in range(2 * nh):
        who = core if k % 2 == 0 else 1 - core
        x_copies.append(
            pltpu.make_async_copy(rows[k], x_ref.at[2 * (k // 2) + who], x_sem.at[k])
        )
    for c in w_copies + x_copies[:2]:
        c.start()

    convs = counts_ref.shape[1]
    each = out_ref.shape[0] // convs
    chunk = 16 * each
    total = acc_ref.shape[0]
    used = total // (each // MAXB)

    @pl.loop(0, convs // 16)
    def _(g):
        i = iota((chunk, 1), 0) + g * chunk
        conv = lax.shift_right_logical(i * (65536 // each + 1), 16)
        inside = i - conv * each
        which = lax.shift_right_logical(inside * (65536 // MAXB + 1), 16)
        slot = inside - which * MAXB
        other = iota((chunk, convs), 1)
        counts = counts_ref[...]
        both = jnp.sum(
            jnp.where(other < conv, counts * 8, jnp.where(other == conv, counts, 0)),
            axis=1,
            keepdims=True,
        )
        start, count = lax.shift_right_logical(both, 3), lax.bitwise_and(both, 7)
        source = jnp.where(slot < count, which * used + start + slot, -1)
        rows_of = pl.ds(pl.multiple_of(g * chunk, chunk), chunk)
        put_ref[rows_of] = (iota((chunk, total), 1) == source).astype(F32).astype(BF16)

    for c in w_copies:
        c.wait()
    half = total // 2
    quarters = (0, -1, 1, -2)
    for s in range(nh):
        for c in x_copies[2 * s : 2 * s + 2]:
            c.wait()
        for c in x_copies[2 * s + 2 : 2 * s + 4]:
            c.start()
        quarter = lax.rem(head + quarters[s] * sign + nh, nh)
        at = pl.multiple_of(quarter * feats, feats)

        @pl.loop(0, 2)
        def _(cc):
            row = pl.ds(pl.multiple_of(cc * half, half), half)
            part = dot(x_ref[2 * s + cc], w_ref[pl.ds(at, feats)])
            if s == 0:
                acc_ref[row] = part
            elif s < nh - 1:
                acc_ref[row] += part
            else:
                acc16_ref[row] = (acc_ref[row] + part).astype(BF16)

    @pl.loop(0, convs // 16)
    def _(g):
        rows_of = pl.ds(pl.multiple_of(g * chunk, chunk), chunk)
        out_ref[rows_of] = dot(put_ref[rows_of], acc16_ref[...]).astype(BF16)


def project(counts, rows, pieces, dims):
    ny, nz, nh, shard = dims
    per, feats = rows[0].shape
    cols = pieces[0].shape[1]
    convs = counts.shape[0]
    each = 2 * (per // USED) * MAXB
    hbm = pl.BlockSpec(memory_space=pl.ANY)
    return pl.pallas_call(
        functools.partial(project_kernel, dims),
        out_shape=jax.ShapeDtypeStruct((convs * each, cols), BF16),
        in_specs=[pl.BlockSpec(memory_space=pltpu.VMEM)] + [hbm] * (2 * nh + PIECES),
        out_specs=pl.BlockSpec(memory_space=pltpu.VMEM),
        scratch_shapes=[
            pltpu.VMEM((nh * feats, cols), BF16),
            pltpu.VMEM((2 * nh, per, feats), BF16),
            pltpu.VMEM((convs * each, 2 * per), BF16),
            pltpu.VMEM((2 * per, cols), F32),
            pltpu.VMEM((2 * per, cols), BF16),
            pltpu.SemaphoreType.DMA((ny * nz * 2,)),
            pltpu.SemaphoreType.DMA((2 * nh,)),
        ],
        compiler_params=pltpu.CompilerParams(vmem_limit_bytes=VMEM_LIMIT),
        cost_estimate=pl.CostEstimate(
            flops=4 * per * nh * feats * cols, bytes_accessed=2 * nh * feats * (cols + 2 * per), transcendentals=0
        ),
        name="project",
    )(counts[None], *rows, *pieces)


def attend_kernel(first, live_ref, q_ref, k_ref, v_ref, nk_ref, nv_ref, *rest):
    out_ref = rest[-1]
    if first:
        out_ref[:, :first] = rest[0][...]
    live = live_ref[0]
    hist = k_ref.shape[0]
    new = nk_ref.shape[0]
    scale = 1.0 / math.sqrt(HD)
    hist_ok = (iota((1, hist), 1) % MAXB) < live
    token = iota((2 * new, new), 0)
    token = jnp.where(token < new, token, token - new)
    new_ok = iota((2 * new, new), 1) <= token

    @pl.loop(0, k_ref.shape[1] // (2 * HD))
    def _(pair):
        lanes = pl.ds(pl.multiple_of(pair * 2 * HD, 2 * HD), 2 * HD)
        all_lanes = pl.ds(pl.multiple_of(first + pair * 2 * HD, 2 * HD), 2 * HD)
        q = q_ref[:, all_lanes] * jnp.asarray(scale, BF16)
        k, v = k_ref[:, lanes], v_ref[:, lanes]
        nk, nv = nk_ref[:, all_lanes], nv_ref[:, all_lanes]
        low = iota(q.shape, 1) < HD
        none = jnp.zeros_like(q)
        q2 = jnp.concatenate([jnp.where(low, q, none), jnp.where(low, none, q)], axis=0)
        sh = jnp.where(hist_ok, dot(q2, k, ((1,), (1,))), -jnp.inf)
        sn = jnp.where(new_ok, dot(q2, nk, ((1,), (1,))), -jnp.inf)
        top = jnp.maximum(
            jnp.max(sh, axis=1, keepdims=True), jnp.max(sn, axis=1, keepdims=True)
        )
        eh, en = jnp.exp(sh - top), jnp.exp(sn - top)
        total = jnp.sum(eh, axis=1, keepdims=True) + jnp.sum(en, axis=1, keepdims=True)
        share = 1.0 / total
        ph, pn = (eh * share).astype(BF16), (en * share).astype(BF16)
        out = dot(ph, v) + dot(pn, nv)
        out_ref[:, all_lanes] = jnp.where(low, out[:new], out[new:]).astype(BF16)


def attend(live, q, k, v, nk, nv, before=None):
    first = 0 if before is None else before.shape[1]
    more = () if before is None else (before,)
    return pl.pallas_call(
        functools.partial(attend_kernel, first),
        out_shape=jax.ShapeDtypeStruct((q.shape[0], first + k.shape[1]), BF16),
        in_specs=[pl.BlockSpec(memory_space=pltpu.SMEM)]
        + [pl.BlockSpec(memory_space=pltpu.VMEM)] * (5 + len(more)),
        out_specs=pl.BlockSpec(memory_space=pltpu.VMEM),
        compiler_params=pltpu.CompilerParams(vmem_limit_bytes=VMEM_LIMIT),
        name="attend",
    )(live, q, k, v, nk, nv, *more)


def ring_step(x, axis, way=1):
    n = lax.axis_size(axis)
    order = (axis, "core") if axis != "head" else ("core", axis)
    place = (lambda i, c: 2 * i + c) if axis != "head" else (lambda i, c: c * n + i)
    perm = []
    for i in range(n):
        perm += [(place(i, 0), place((i + way) % n, 0)), (place(i, 1), place((i - way) % n, 1))]
    return lax.ppermute(x, order, perm)


def gather_rows(own):
    behind = ring_step(own, "head")
    ahead = ring_step(own, "head", -1)
    opposite = ring_step(behind, "head")
    return [
        own, swap_cores(own),
        behind, swap_cores(ahead),
        ahead, swap_cores(behind),
        opposite, swap_cores(opposite),
    ]


def swap_cores(x):
    return lax.ppermute(x, "core", [(0, 1), (1, 0)])


def kinds(x):
    half = x.shape[0] // 2
    return x[:half], x[half:]


def gather_weights(key_weight, value_weight):
    upper = lax.axis_index("core") == 0
    mine = jnp.where(upper, key_weight, value_weight)
    other = jnp.where(upper, value_weight, key_weight)
    own = jnp.concatenate([mine, other])
    near = swap_cores(jnp.concatenate([other, mine]))
    zero = jnp.where(upper, own, near)
    one = jnp.where(upper, near, own)

    y1 = ring_step(zero, "y")
    y2 = ring_step(kinds(y1)[0], "y")
    got = swap_cores(jnp.concatenate([y1, y2]))
    n = key_weight.shape[0]
    group = jnp.concatenate(
        [
            kinds(zero)[0], kinds(y1)[0], got[n : 2 * n], y2,
            kinds(zero)[1], kinds(y1)[1], got[:n], got[2 * n :],
        ]
    )
    z1 = ring_step(group, "z")
    z2 = ring_step(z1, "z")
    z3 = ring_step(z2, "z")
    z4 = ring_step(kinds(z3)[0], "z")
    across = [swap_cores(kinds(t)[1]) for t in (z1, z2, z3)]
    first = [group, z1, z2, z3, z4] + across

    r1 = ring_step(one, "z")
    r2 = ring_step(r1, "z")
    r3 = ring_step(r2, "z")
    r4 = ring_step(kinds(r3)[0], "z")
    ring = [one, r1, r2, r3]
    got = swap_cores(jnp.concatenate([r1, r2, r3, r4]))
    line = jnp.concatenate(
        [kinds(t)[0] for t in ring]
        + [got[(2 * k + 1) * n : (2 * k + 2) * n] for k in range(3)]
        + [r4]
        + [kinds(t)[1] for t in ring]
        + [got[2 * k * n : (2 * k + 1) * n] for k in range(3)]
        + [got[6 * n :]]
    )
    l1 = ring_step(line, "y")
    l2 = ring_step(kinds(l1)[0], "y")
    second = [line, l1, l2, swap_cores(kinds(l1)[1])]
    return first + second


def per_device(queries, new_keys, new_values, pool, block_table, block_counts, key_weight, value_weight):
    ny, nz, nh = lax.axis_size("y"), lax.axis_size("z"), lax.axis_size("head")
    live = live_rows(block_counts, block_table, pool)
    live = live.reshape(-1, live.shape[2])
    rows = gather_rows(live)

    pieces = gather_weights(key_weight, value_weight)
    dims = (ny, nz, nh, key_weight.shape[0])
    sent = project(block_counts, rows, pieces, dims)
    convs = block_counts.shape[0]
    sent = sent.reshape(convs, -1, sent.shape[1])
    got = lax.all_to_all(sent, PLANE, split_axis=0, concat_axis=0, tiled=True)
    got = got.reshape(convs // 2, 2, got.shape[1], got.shape[2])
    keys = got[:, 0].reshape(-1, got.shape[3])
    values = got[:, 1].reshape(-1, got.shape[3])
    mine = lax.axis_index(PLANE)
    count = lax.dynamic_slice(block_counts, (mine,), (1,))
    return attend(count, queries[0], keys, values, new_keys[0], new_values[0])[None]


def solution(mesh):
    grid = Mesh(mesh.devices.reshape(GRID + (mesh.devices.shape[1],)), PLANE + ("head",))
    return jax.shard_map(
        per_device,
        mesh=grid,
        in_specs=(
            P(PLANE, None, "head"),
            P(PLANE, None, "head"),
            P(PLANE, None, "head"),
            P(None, PLANE, "head"),
            P(),
            P(),
            P(PLANE, "head"),
            P(PLANE, "head"),
        ),
        out_specs=P(PLANE, None, "head"),
        check_vma=False,
    )
```

```python
import functools
import math

import jax
import jax.numpy as jnp
from jax import lax
from jax.experimental import pallas as pl
from jax.experimental.pallas import tpu as pltpu
from jax.sharding import Mesh, PartitionSpec as P

HD = 64
MAXB = 6
USED = 224
GRID = (4, 8, 2)
PLANE = ("y", "z", "core")
BF16 = jnp.bfloat16
F32 = jnp.float32
VMEM_LIMIT = 56 * 1024 * 1024


def dot(a, b, contract=((1,), (0,))):
    return lax.dot_general(a, b, (contract, ((), ())), preferred_element_type=F32)


def iota(shape, dim):
    return lax.broadcasted_iota(jnp.int32, shape, dim)


def live_rows_kernel(counts_ref, table_ref, pool_ref, out_ref):
    convs = counts_ref.shape[1]
    slots = table_ref.shape[1]
    parities, blocks, _ = pool_ref.shape
    used = out_ref.shape[1]
    counts = jnp.broadcast_to(counts_ref[...].astype(F32), (8, convs)).astype(BF16)
    conv_of = iota((convs, slots), 1) // MAXB
    conv_row = iota((convs, slots), 0)
    count_k = dot(counts, (conv_row == conv_of).astype(F32).astype(BF16))[0:1]
    start_k = dot(counts, (conv_row < conv_of).astype(F32).astype(BF16))[0:1]
    slot_k = iota((1, slots), 1) % MAXB
    count_k = count_k.astype(jnp.int32)
    place_k = jnp.where(slot_k < count_k, start_k.astype(jnp.int32) + slot_k, -1)
    takes = (iota((used, slots), 0) == place_k).astype(F32).astype(BF16)
    names = (iota((blocks, slots), 0) == table_ref[...]).astype(F32).astype(BF16)
    pick = dot(takes, names, ((1,), (1,))).astype(BF16)
    for r in range(parities):
        out_ref[r] = dot(pick, pool_ref[r]).astype(BF16)


def live_rows(counts, table, pool):
    blocks, parities, feats = pool.shape
    return pl.pallas_call(
        live_rows_kernel,
        out_shape=jax.ShapeDtypeStruct((parities, USED, feats), BF16),
        in_specs=[pl.BlockSpec(memory_space=pltpu.VMEM)] * 3,
        out_specs=pl.BlockSpec(memory_space=pltpu.VMEM),
        compiler_params=pltpu.CompilerParams(vmem_limit_bytes=VMEM_LIMIT),
        name="live_rows",
    )(counts[None], table[None], jnp.transpose(pool, (1, 0, 2)))


def piece_table(ny, nz):
    table = []
    dys = (0, -1, 1, -2)
    dzs = (0, -1, -2, -3, 1, 2, 3, -4)
    for s in range(5):
        for j, dy in enumerate(dys):
            table.append((s, j, dy, -s, 0))
    for s in range(1, 4):
        for j, dy in enumerate(dys):
            table.append((4 + s, j, -dy, s, 0))
    for s in range(3):
        for j, dz in enumerate(dzs):
            table.append((8 + s, j, -s, dz, 1))
    for j, dz in enumerate(dzs):
        table.append((11, j, 1, -dz, 1))
    assert len(table) == ny * nz * 2
    return table


PIECES = 12


def project_kernel(dims, counts_ref, *rest):
    ny, nz, nh, shard = dims
    rows = rest[: 2 * nh]
    pieces = rest[2 * nh : 2 * nh + PIECES]
    out_ref, w_ref, x_ref, put_ref, acc_ref, acc16_ref, w_sem, x_sem = rest[2 * nh + PIECES :]
    y, z, core = (lax.axis_index(a) for a in PLANE)
    head = lax.axis_index("head")
    sign = 1 - 2 * core
    cols = w_ref.shape[1]
    feats = w_ref.shape[0] // nh

    quarters = (0, -1, 1, -2)
    table = piece_table(ny, nz)

    def plane_of(s):
        return lax.rem(y + quarters[s] * sign + ny, ny)

    def copies(s, rows_from):
        group = []
        for k, (src, part, dy, dz, owner) in enumerate(table):
            if (dy - quarters[s]) % ny:
                continue
            chip = plane_of(s) * nz + lax.rem(z + dz * sign + nz, nz)
            at = pl.multiple_of((chip * 2 + owner) * shard, shard)
            group.append(
                pltpu.make_async_copy(
                    pieces[src].at[pl.ds(part * shard, shard)],
                    w_ref.at[pl.ds(at, shard)],
                    w_sem.at[k],
                )
            )
        both = [
            pltpu.make_async_copy(
                rows[2 * rows_from + c], x_ref.at[2 * s + (core if c == 0 else 1 - core)], x_sem.at[2 * s + c]
            )
            for c in range(2)
        ]
        return group, both

    def start(s):
        for c in copies(s, 0)[0]:
            c.start()
        for k in range(nh):

            @pl.when(lax.rem(head + quarters[k] * sign + nh, nh) == plane_of(s))
            def _():
                for c in copies(s, k)[1]:
                    c.start()

    start(0)

    convs = counts_ref.shape[1]
    each = out_ref.shape[0] // convs
    chunk = 16 * each
    total = acc_ref.shape[0]
    used = total // (each // MAXB)

    @pl.loop(0, convs // 16)
    def _(g):
        i = iota((chunk, 1), 0) + g * chunk
        conv = lax.shift_right_logical(i * (65536 // each + 1), 16)
        inside = i - conv * each
        which = lax.shift_right_logical(inside * (65536 // MAXB + 1), 16)
        slot = inside - which * MAXB
        other = iota((chunk, convs), 1)
        counts = counts_ref[...]
        both = jnp.sum(
            jnp.where(other < conv, counts * 8, jnp.where(other == conv, counts, 0)),
            axis=1,
            keepdims=True,
        )
        start, count = lax.shift_right_logical(both, 3), lax.bitwise_and(both, 7)
        source = jnp.where(slot < count, which * used + start + slot, -1)
        rows_of = pl.ds(pl.multiple_of(g * chunk, chunk), chunk)
        put_ref[rows_of] = (iota((chunk, total), 1) == source).astype(F32).astype(BF16)

    start(1)
    half = total // 2
    for s in range(nh):
        group, both = copies(s, 0)
        for c in group + both:
            c.wait()
        if s + 2 < nh:
            start(s + 2)
        at = pl.multiple_of(plane_of(s) * feats, feats)

        @pl.loop(0, 2)
        def _(cc):
            row = pl.ds(pl.multiple_of(cc * half, half), half)
            part = dot(x_ref[2 * s + cc], w_ref[pl.ds(at, feats)])
            if s == 0:
                acc_ref[row] = part
            elif s < nh - 1:
                acc_ref[row] += part
            else:
                acc16_ref[row] = (acc_ref[row] + part).astype(BF16)

    @pl.loop(0, convs // 16)
    def _(g):
        rows_of = pl.ds(pl.multiple_of(g * chunk, chunk), chunk)
        out_ref[rows_of] = dot(put_ref[rows_of], acc16_ref[...]).astype(BF16)


def project(counts, rows, pieces, dims):
    ny, nz, nh, shard = dims
    per, feats = rows[0].shape
    cols = pieces[0].shape[1]
    convs = counts.shape[0]
    each = 2 * (per // USED) * MAXB
    hbm = pl.BlockSpec(memory_space=pl.ANY)
    return pl.pallas_call(
        functools.partial(project_kernel, dims),
        out_shape=jax.ShapeDtypeStruct((convs * each, cols), BF16),
        in_specs=[pl.BlockSpec(memory_space=pltpu.VMEM)] + [hbm] * (2 * nh + PIECES),
        out_specs=pl.BlockSpec(memory_space=pltpu.VMEM),
        scratch_shapes=[
            pltpu.VMEM((nh * feats, cols), BF16),
            pltpu.VMEM((2 * nh, per, feats), BF16),
            pltpu.VMEM((convs * each, 2 * per), BF16),
            pltpu.VMEM((2 * per, cols), F32),
            pltpu.VMEM((2 * per, cols), BF16),
            pltpu.SemaphoreType.DMA((ny * nz * 2,)),
            pltpu.SemaphoreType.DMA((2 * nh,)),
        ],
        compiler_params=pltpu.CompilerParams(vmem_limit_bytes=VMEM_LIMIT),
        cost_estimate=pl.CostEstimate(
            flops=4 * per * nh * feats * cols, bytes_accessed=2 * nh * feats * (cols + 2 * per), transcendentals=0
        ),
        name="project",
    )(counts[None], *rows, *pieces)


def attend_kernel(first, live_ref, q_ref, k_ref, v_ref, nk_ref, nv_ref, *rest):
    out_ref = rest[-1]
    if first:
        out_ref[:, :first] = rest[0][...]
    live = live_ref[0]
    hist = k_ref.shape[0]
    new = nk_ref.shape[0]
    scale = 1.0 / math.sqrt(HD)
    hist_ok = (iota((1, hist), 1) % MAXB) < live
    token = iota((2 * new, new), 0)
    token = jnp.where(token < new, token, token - new)
    new_ok = iota((2 * new, new), 1) <= token

    @pl.loop(0, k_ref.shape[1] // (2 * HD))
    def _(pair):
        lanes = pl.ds(pl.multiple_of(pair * 2 * HD, 2 * HD), 2 * HD)
        all_lanes = pl.ds(pl.multiple_of(first + pair * 2 * HD, 2 * HD), 2 * HD)
        q = q_ref[:, all_lanes] * jnp.asarray(scale, BF16)
        k, v = k_ref[:, lanes], v_ref[:, lanes]
        nk, nv = nk_ref[:, all_lanes], nv_ref[:, all_lanes]
        low = iota(q.shape, 1) < HD
        none = jnp.zeros_like(q)
        q2 = jnp.concatenate([jnp.where(low, q, none), jnp.where(low, none, q)], axis=0)
        sh = jnp.where(hist_ok, dot(q2, k, ((1,), (1,))), -jnp.inf)
        sn = jnp.where(new_ok, dot(q2, nk, ((1,), (1,))), -jnp.inf)
        top = jnp.maximum(
            jnp.max(sh, axis=1, keepdims=True), jnp.max(sn, axis=1, keepdims=True)
        )
        eh, en = jnp.exp(sh - top), jnp.exp(sn - top)
        total = jnp.sum(eh, axis=1, keepdims=True) + jnp.sum(en, axis=1, keepdims=True)
        share = 1.0 / total
        ph, pn = (eh * share).astype(BF16), (en * share).astype(BF16)
        out = dot(ph, v) + dot(pn, nv)
        out_ref[:, all_lanes] = jnp.where(low, out[:new], out[new:]).astype(BF16)


def attend(live, q, k, v, nk, nv, before=None):
    first = 0 if before is None else before.shape[1]
    more = () if before is None else (before,)
    return pl.pallas_call(
        functools.partial(attend_kernel, first),
        out_shape=jax.ShapeDtypeStruct((q.shape[0], first + k.shape[1]), BF16),
        in_specs=[pl.BlockSpec(memory_space=pltpu.SMEM)]
        + [pl.BlockSpec(memory_space=pltpu.VMEM)] * (5 + len(more)),
        out_specs=pl.BlockSpec(memory_space=pltpu.VMEM),
        compiler_params=pltpu.CompilerParams(vmem_limit_bytes=VMEM_LIMIT),
        name="attend",
    )(live, q, k, v, nk, nv, *more)


def ring_step(x, axis, way=1):
    n = lax.axis_size(axis)
    order = (axis, "core") if axis != "head" else ("core", axis)
    place = (lambda i, c: 2 * i + c) if axis != "head" else (lambda i, c: c * n + i)
    perm = []
    for i in range(n):
        perm += [(place(i, 0), place((i + way) % n, 0)), (place(i, 1), place((i - way) % n, 1))]
    return lax.ppermute(x, order, perm)


def gather_rows(own):
    behind = ring_step(own, "head")
    ahead = ring_step(own, "head", -1)
    opposite = ring_step(behind, "head")
    return [
        own, swap_cores(own),
        behind, swap_cores(ahead),
        ahead, swap_cores(behind),
        opposite, swap_cores(opposite),
    ]


def swap_cores(x):
    return lax.ppermute(x, "core", [(0, 1), (1, 0)])


def kinds(x):
    half = x.shape[0] // 2
    return x[:half], x[half:]


def gather_weights(key_weight, value_weight):
    upper = lax.axis_index("core") == 0
    mine = jnp.where(upper, key_weight, value_weight)
    other = jnp.where(upper, value_weight, key_weight)
    own = jnp.concatenate([mine, other])
    near = swap_cores(jnp.concatenate([other, mine]))
    zero = jnp.where(upper, own, near)
    one = jnp.where(upper, near, own)

    y1 = ring_step(zero, "y")
    y2 = ring_step(kinds(y1)[0], "y")
    got = swap_cores(jnp.concatenate([y1, y2]))
    n = key_weight.shape[0]
    group = jnp.concatenate(
        [
            kinds(zero)[0], kinds(y1)[0], got[n : 2 * n], y2,
            kinds(zero)[1], kinds(y1)[1], got[:n], got[2 * n :],
        ]
    )
    z1 = ring_step(group, "z")
    z2 = ring_step(z1, "z")
    z3 = ring_step(z2, "z")
    z4 = ring_step(kinds(z3)[0], "z")
    across = [swap_cores(kinds(t)[1]) for t in (z1, z2, z3)]
    first = [group, z1, z2, z3, z4] + across

    r1 = ring_step(one, "z")
    r2 = ring_step(r1, "z")
    r3 = ring_step(r2, "z")
    r4 = ring_step(kinds(r3)[0], "z")
    ring = [one, r1, r2, r3]
    got = swap_cores(jnp.concatenate([r1, r2, r3, r4]))
    line = jnp.concatenate(
        [kinds(t)[0] for t in ring]
        + [got[(2 * k + 1) * n : (2 * k + 2) * n] for k in range(3)]
        + [r4]
        + [kinds(t)[1] for t in ring]
        + [got[2 * k * n : (2 * k + 1) * n] for k in range(3)]
        + [got[6 * n :]]
    )
    l1 = ring_step(line, "y")
    l2 = ring_step(kinds(l1)[0], "y")
    second = [line, l1, l2, swap_cores(kinds(l1)[1])]
    return first + second


def per_device(queries, new_keys, new_values, pool, block_table, block_counts, key_weight, value_weight):
    ny, nz, nh = lax.axis_size("y"), lax.axis_size("z"), lax.axis_size("head")
    live = live_rows(block_counts, block_table, pool)
    live = live.reshape(-1, live.shape[2])
    rows = gather_rows(live)

    pieces = gather_weights(key_weight, value_weight)
    dims = (ny, nz, nh, key_weight.shape[0])
    sent = project(block_counts, rows, pieces, dims)
    convs = block_counts.shape[0]
    sent = sent.reshape(convs, -1, sent.shape[1])
    got = lax.all_to_all(sent, PLANE, split_axis=0, concat_axis=0, tiled=True)
    got = got.reshape(convs // 2, 2, got.shape[1], got.shape[2])
    keys = got[:, 0].reshape(-1, got.shape[3])
    values = got[:, 1].reshape(-1, got.shape[3])
    mine = lax.axis_index(PLANE)
    count = lax.dynamic_slice(block_counts, (mine,), (1,))
    return attend(count, queries[0], keys, values, new_keys[0], new_values[0])[None]


def solution(mesh):
    grid = Mesh(mesh.devices.reshape(GRID + (mesh.devices.shape[1],)), PLANE + ("head",))
    return jax.shard_map(
        per_device,
        mesh=grid,
        in_specs=(
            P(PLANE, None, "head"),
            P(PLANE, None, "head"),
            P(PLANE, None, "head"),
            P(None, PLANE, "head"),
            P(),
            P(),
            P(PLANE, "head"),
            P(PLANE, "head"),
        ),
        out_specs=P(PLANE, None, "head"),
        check_vma=False,
    )
```

```python
import functools
import math

import jax
import jax.numpy as jnp
from jax import lax
from jax.experimental import pallas as pl
from jax.experimental.pallas import tpu as pltpu
from jax.sharding import Mesh, PartitionSpec as P

HD = 64
MAXB = 6
USED = 224
GRID = (4, 8, 2)
PLANE = ("y", "z", "core")
BF16 = jnp.bfloat16
F32 = jnp.float32
VMEM_LIMIT = 56 * 1024 * 1024


def dot(a, b, contract=((1,), (0,))):
    return lax.dot_general(a, b, (contract, ((), ())), preferred_element_type=F32)


def iota(shape, dim):
    return lax.broadcasted_iota(jnp.int32, shape, dim)


def live_rows_kernel(counts_ref, table_ref, pool_ref, out_ref):
    convs = counts_ref.shape[1]
    slots = table_ref.shape[1]
    parities, blocks, _ = pool_ref.shape
    used = out_ref.shape[1]
    counts = jnp.broadcast_to(counts_ref[...].astype(F32), (8, convs)).astype(BF16)
    conv_of = iota((convs, slots), 1) // MAXB
    conv_row = iota((convs, slots), 0)
    count_k = dot(counts, (conv_row == conv_of).astype(F32).astype(BF16))[0:1]
    start_k = dot(counts, (conv_row < conv_of).astype(F32).astype(BF16))[0:1]
    slot_k = iota((1, slots), 1) % MAXB
    count_k = count_k.astype(jnp.int32)
    place_k = jnp.where(slot_k < count_k, start_k.astype(jnp.int32) + slot_k, -1)
    takes = (iota((used, slots), 0) == place_k).astype(F32).astype(BF16)
    names = (iota((blocks, slots), 0) == table_ref[...]).astype(F32).astype(BF16)
    pick = dot(takes, names, ((1,), (1,))).astype(BF16)
    for r in range(parities):
        out_ref[r] = dot(pick, pool_ref[r]).astype(BF16)


def live_rows(counts, table, pool):
    blocks, parities, feats = pool.shape
    return pl.pallas_call(
        live_rows_kernel,
        out_shape=jax.ShapeDtypeStruct((parities, USED, feats), BF16),
        in_specs=[pl.BlockSpec(memory_space=pltpu.VMEM)] * 3,
        out_specs=pl.BlockSpec(memory_space=pltpu.VMEM),
        compiler_params=pltpu.CompilerParams(vmem_limit_bytes=VMEM_LIMIT),
        name="live_rows",
    )(counts[None], table[None], jnp.transpose(pool, (1, 0, 2)))


def piece_table(ny, nz):
    table = []
    dys = (0, -1, 1, -2)
    dzs = (0, -1, -2, -3, 1, 2, 3, -4)
    for s in range(5):
        for j, dy in enumerate(dys):
            table.append((s, j, dy, -s, 0))
    for s in range(1, 4):
        for j, dy in enumerate(dys):
            table.append((4 + s, j, -dy, s, 0))
    for s in range(3):
        for j, dz in enumerate(dzs):
            table.append((8 + s, j, -s, dz, 1))
    for j, dz in enumerate(dzs):
        table.append((11, j, 1, -dz, 1))
    assert len(table) == ny * nz * 2
    return table


PIECES = 12


def project_kernel(dims, counts_ref, *rest):
    ny, nz, nh, shard = dims
    rows = rest[: 2 * nh]
    pieces = rest[2 * nh : 2 * nh + PIECES]
    out_ref, w_ref, x_ref, put_ref, acc_ref, acc16_ref, w_sem, x_sem = rest[2 * nh + PIECES :]
    y, z, core = (lax.axis_index(a) for a in PLANE)
    head = lax.axis_index("head")
    sign = 1 - 2 * core
    cols = w_ref.shape[1]
    feats = w_ref.shape[0] // nh

    quarters = (0, -1, 1, -2)
    table = piece_table(ny, nz)

    def plane_of(s):
        return lax.rem(y + quarters[s] * sign + ny, ny)

    def copies(s, rows_from):
        group = []
        for k, (src, part, dy, dz, owner) in enumerate(table):
            if (dy - quarters[s]) % ny:
                continue
            chip = plane_of(s) * nz + lax.rem(z + dz * sign + nz, nz)
            at = pl.multiple_of((chip * 2 + owner) * shard, shard)
            group.append(
                pltpu.make_async_copy(
                    pieces[src].at[pl.ds(part * shard, shard)],
                    w_ref.at[pl.ds(at, shard)],
                    w_sem.at[k],
                )
            )
        both = [
            pltpu.make_async_copy(
                rows[2 * rows_from + c], x_ref.at[2 * s + (core if c == 0 else 1 - core)], x_sem.at[2 * s + c]
            )
            for c in range(2)
        ]
        return group, both

    def start(s):
        for c in copies(s, 0)[0]:
            c.start()
        for k in range(nh):

            @pl.when(lax.rem(head + quarters[k] * sign + nh, nh) == plane_of(s))
            def _():
                for c in copies(s, k)[1]:
                    c.start()

    start(0)

    convs = counts_ref.shape[1]
    each = out_ref.shape[0] // convs
    chunk = 16 * each
    total = acc_ref.shape[0]
    used = total // (each // MAXB)

    @pl.loop(0, convs // 16)
    def _(g):
        i = iota((chunk, 1), 0) + g * chunk
        conv = lax.shift_right_logical(i * (65536 // each + 1), 16)
        inside = i - conv * each
        which = lax.shift_right_logical(inside * (65536 // MAXB + 1), 16)
        slot = inside - which * MAXB
        other = iota((chunk, convs), 1)
        counts = counts_ref[...]
        both = jnp.sum(
            jnp.where(other < conv, counts * 8, jnp.where(other == conv, counts, 0)),
            axis=1,
            keepdims=True,
        )
        start, count = lax.shift_right_logical(both, 3), lax.bitwise_and(both, 7)
        source = jnp.where(slot < count, which * used + start + slot, -1)
        rows_of = pl.ds(pl.multiple_of(g * chunk, chunk), chunk)
        put_ref[rows_of] = (iota((chunk, total), 1) == source).astype(F32).astype(BF16)

    start(1)
    half = total // 2
    for s in range(nh):
        group, both = copies(s, 0)
        for c in group + both:
            c.wait()
        if s + 2 < nh:
            start(s + 2)
        at = pl.multiple_of(plane_of(s) * feats, feats)

        @pl.loop(0, 2)
        def _(cc):
            row = pl.ds(pl.multiple_of(cc * half, half), half)
            part = dot(x_ref[2 * s + cc], w_ref[pl.ds(at, feats)])
            if s == 0:
                acc_ref[row] = part
            elif s < nh - 1:
                acc_ref[row] += part
            else:
                acc16_ref[row] = (acc_ref[row] + part).astype(BF16)

    @pl.loop(0, convs // 16)
    def _(g):
        rows_of = pl.ds(pl.multiple_of(g * chunk, chunk), chunk)
        out_ref[rows_of] = dot(put_ref[rows_of], acc16_ref[...]).astype(BF16)


def project(counts, rows, pieces, dims):
    ny, nz, nh, shard = dims
    per, feats = rows[0].shape
    cols = pieces[0].shape[1]
    convs = counts.shape[0]
    each = 2 * (per // USED) * MAXB
    hbm = pl.BlockSpec(memory_space=pl.ANY)
    return pl.pallas_call(
        functools.partial(project_kernel, dims),
        out_shape=jax.ShapeDtypeStruct((convs * each, cols), BF16),
        in_specs=[pl.BlockSpec(memory_space=pltpu.VMEM)] + [hbm] * (2 * nh + PIECES),
        out_specs=pl.BlockSpec(memory_space=pltpu.VMEM),
        scratch_shapes=[
            pltpu.VMEM((nh * feats, cols), BF16),
            pltpu.VMEM((2 * nh, per, feats), BF16),
            pltpu.VMEM((convs * each, 2 * per), BF16),
            pltpu.VMEM((2 * per, cols), F32),
            pltpu.VMEM((2 * per, cols), BF16),
            pltpu.SemaphoreType.DMA((ny * nz * 2,)),
            pltpu.SemaphoreType.DMA((2 * nh,)),
        ],
        compiler_params=pltpu.CompilerParams(vmem_limit_bytes=VMEM_LIMIT),
        cost_estimate=pl.CostEstimate(
            flops=4 * per * nh * feats * cols, bytes_accessed=2 * nh * feats * (cols + 2 * per), transcendentals=0
        ),
        name="project",
    )(counts[None], *rows, *pieces)


def attend_kernel(first, live_ref, q_ref, k_ref, v_ref, nk_ref, nv_ref, *rest):
    out_ref = rest[-1]
    if first:
        out_ref[:, :first] = rest[0][...]
    live = live_ref[0]
    hist = k_ref.shape[0]
    new = nk_ref.shape[0]
    scale = 1.0 / math.sqrt(HD)
    hist_ok = (iota((1, hist), 1) % MAXB) < live
    token = iota((2 * new, new), 0)
    token = jnp.where(token < new, token, token - new)
    new_ok = iota((2 * new, new), 1) <= token

    @pl.loop(0, k_ref.shape[1] // (2 * HD), unroll=2)
    def _(pair):
        lanes = pl.ds(pl.multiple_of(pair * 2 * HD, 2 * HD), 2 * HD)
        all_lanes = pl.ds(pl.multiple_of(first + pair * 2 * HD, 2 * HD), 2 * HD)
        q = q_ref[:, all_lanes] * jnp.asarray(scale, BF16)
        k, v = k_ref[:, lanes], v_ref[:, lanes]
        nk, nv = nk_ref[:, all_lanes], nv_ref[:, all_lanes]
        low = iota(q.shape, 1) < HD
        none = jnp.zeros_like(q)
        q2 = jnp.concatenate([jnp.where(low, q, none), jnp.where(low, none, q)], axis=0)
        sh = jnp.where(hist_ok, dot(q2, k, ((1,), (1,))), -jnp.inf)
        sn = jnp.where(new_ok, dot(q2, nk, ((1,), (1,))), -jnp.inf)
        top = jnp.maximum(
            jnp.max(sh, axis=1, keepdims=True), jnp.max(sn, axis=1, keepdims=True)
        )
        eh, en = jnp.exp(sh - top), jnp.exp(sn - top)
        total = jnp.sum(eh, axis=1, keepdims=True) + jnp.sum(en, axis=1, keepdims=True)
        share = 1.0 / total
        ph, pn = (eh * share).astype(BF16), (en * share).astype(BF16)
        out = dot(ph, v) + dot(pn, nv)
        out_ref[:, all_lanes] = jnp.where(low, out[:new], out[new:]).astype(BF16)


def attend(live, q, k, v, nk, nv, before=None):
    first = 0 if before is None else before.shape[1]
    more = () if before is None else (before,)
    return pl.pallas_call(
        functools.partial(attend_kernel, first),
        out_shape=jax.ShapeDtypeStruct((q.shape[0], first + k.shape[1]), BF16),
        in_specs=[pl.BlockSpec(memory_space=pltpu.SMEM)]
        + [pl.BlockSpec(memory_space=pltpu.VMEM)] * (5 + len(more)),
        out_specs=pl.BlockSpec(memory_space=pltpu.VMEM),
        compiler_params=pltpu.CompilerParams(vmem_limit_bytes=VMEM_LIMIT),
        name="attend",
    )(live, q, k, v, nk, nv, *more)


def ring_step(x, axis, way=1):
    n = lax.axis_size(axis)
    order = (axis, "core") if axis != "head" else ("core", axis)
    place = (lambda i, c: 2 * i + c) if axis != "head" else (lambda i, c: c * n + i)
    perm = []
    for i in range(n):
        perm += [(place(i, 0), place((i + way) % n, 0)), (place(i, 1), place((i - way) % n, 1))]
    return lax.ppermute(x, order, perm)


def gather_rows(own):
    behind = ring_step(own, "head")
    ahead = ring_step(own, "head", -1)
    opposite = ring_step(behind, "head")
    return [
        own, swap_cores(own),
        behind, swap_cores(ahead),
        ahead, swap_cores(behind),
        opposite, swap_cores(opposite),
    ]


def swap_cores(x):
    return lax.ppermute(x, "core", [(0, 1), (1, 0)])


def kinds(x):
    half = x.shape[0] // 2
    return x[:half], x[half:]


def gather_weights(key_weight, value_weight):
    upper = lax.axis_index("core") == 0
    mine = jnp.where(upper, key_weight, value_weight)
    other = jnp.where(upper, value_weight, key_weight)
    own = jnp.concatenate([mine, other])
    near = swap_cores(jnp.concatenate([other, mine]))
    zero = jnp.where(upper, own, near)
    one = jnp.where(upper, near, own)

    y1 = ring_step(zero, "y")
    y2 = ring_step(kinds(y1)[0], "y")
    got = swap_cores(jnp.concatenate([y1, y2]))
    n = key_weight.shape[0]
    group = jnp.concatenate(
        [
            kinds(zero)[0], kinds(y1)[0], got[n : 2 * n], y2,
            kinds(zero)[1], kinds(y1)[1], got[:n], got[2 * n :],
        ]
    )
    z1 = ring_step(group, "z")
    z2 = ring_step(z1, "z")
    z3 = ring_step(z2, "z")
    z4 = ring_step(kinds(z3)[0], "z")
    across = [swap_cores(kinds(t)[1]) for t in (z1, z2, z3)]
    first = [group, z1, z2, z3, z4] + across

    r1 = ring_step(one, "z")
    r2 = ring_step(r1, "z")
    r3 = ring_step(r2, "z")
    r4 = ring_step(kinds(r3)[0], "z")
    ring = [one, r1, r2, r3]
    got = swap_cores(jnp.concatenate([r1, r2, r3, r4]))
    line = jnp.concatenate(
        [kinds(t)[0] for t in ring]
        + [got[(2 * k + 1) * n : (2 * k + 2) * n] for k in range(3)]
        + [r4]
        + [kinds(t)[1] for t in ring]
        + [got[2 * k * n : (2 * k + 1) * n] for k in range(3)]
        + [got[6 * n :]]
    )
    l1 = ring_step(line, "y")
    l2 = ring_step(kinds(l1)[0], "y")
    second = [line, l1, l2, swap_cores(kinds(l1)[1])]
    return first + second


def per_device(queries, new_keys, new_values, pool, block_table, block_counts, key_weight, value_weight):
    ny, nz, nh = lax.axis_size("y"), lax.axis_size("z"), lax.axis_size("head")
    live = live_rows(block_counts, block_table, pool)
    live = live.reshape(-1, live.shape[2])
    rows = gather_rows(live)

    pieces = gather_weights(key_weight, value_weight)
    dims = (ny, nz, nh, key_weight.shape[0])
    sent = project(block_counts, rows, pieces, dims)
    convs = block_counts.shape[0]
    sent = sent.reshape(convs, -1, sent.shape[1])
    got = lax.all_to_all(sent, PLANE, split_axis=0, concat_axis=0, tiled=True)
    got = got.reshape(convs // 2, 2, got.shape[1], got.shape[2])
    keys = got[:, 0].reshape(-1, got.shape[3])
    values = got[:, 1].reshape(-1, got.shape[3])
    mine = lax.axis_index(PLANE)
    count = lax.dynamic_slice(block_counts, (mine,), (1,))
    return attend(count, queries[0], keys, values, new_keys[0], new_values[0])[None]


def solution(mesh):
    grid = Mesh(mesh.devices.reshape(GRID + (mesh.devices.shape[1],)), PLANE + ("head",))
    return jax.shard_map(
        per_device,
        mesh=grid,
        in_specs=(
            P(PLANE, None, "head"),
            P(PLANE, None, "head"),
            P(PLANE, None, "head"),
            P(None, PLANE, "head"),
            P(),
            P(),
            P(PLANE, "head"),
            P(PLANE, "head"),
        ),
        out_specs=P(PLANE, None, "head"),
        check_vma=False,
    )
```
